32 devices in a mesh: fsdp: 8 (over z, x), tp: 4 (over y, core).
Axes of the slice: x: 2, y: 2, z: 4, core: 2. Of those that a mesh axis runs over, the one named last changes fastest.
Arguments:
- inputs: bfloat16 [8192, 2048], P(('fsdp', 'tp')), may hold values from -6 to 6
- segments: int32 [8, 1024], P('fsdp'), may hold values from 0 to 1, as said below
- ln_gain: bfloat16 [2048], replicated, may hold values from 0.099609375 to 1.8984375
- ln_bias: bfloat16 [2048], replicated, may hold values from -4 to 4
- w_qkv: bfloat16 [3, 2048, 2048], P(None, 'fsdp', 'tp'), may hold values from -0.1875 to 0.1875
- b_qkv: bfloat16 [3, 2048], P(None, 'tp'), may hold values from -6 to 6
- w_out: bfloat16 [2048, 2048], P('tp', 'fsdp'), may hold values from -0.5 to 0.5
- b_out: bfloat16 [2048], replicated, may hold values from -4 to 4
- w_fc1: bfloat16 [2048, 8192], P('fsdp', 'tp'), may hold values from -0.125 to 0.125
- b_fc1: bfloat16 [8192], P('tp'), may hold values from -6 to 6
- w_fc2: bfloat16 [8192, 2048], P('tp', 'fsdp'), may hold values from -0.0625 to 0.0625
- b_fc2: bfloat16 [2048], replicated, may hold values from -4 to 4
- cotangent: bfloat16 [8192, 2048], P(('fsdp', 'tp')), may hold values from -6 to 6
Outputs:
- outputs: bfloat16 [8192, 2048], P(('fsdp', 'tp'))
- grad_inputs: float32 [8192, 2048], P(('fsdp', 'tp'))
- grad_ln_gain: float32 [2048], replicated
- grad_ln_bias: float32 [2048], replicated
- grad_w_qkv: float32 [3, 2048, 2048], P(None, 'fsdp', 'tp')
- grad_b_qkv: float32 [3, 2048], replicated
- grad_w_out: float32 [2048, 2048], P('tp', 'fsdp')
- grad_b_out: float32 [2048], replicated
- grad_w_fc1: float32 [2048, 8192], P('fsdp', 'tp')
- grad_b_fc1: float32 [8192], replicated
- grad_w_fc2: float32 [8192, 2048], P('tp', 'fsdp')
- grad_b_fc2: float32 [2048], replicated
The draws below stay inside these ranges and needn't reach their ends.
Inputs may be any that keep to these rules, and one draw needn't show every extreme that they name: `segments`: each row never falls and holds documents 0 and 1; document 1 starts at a position from 204 to 255 or from 769 to 820.
All inputs are finite; a program needn't handle non-finite values.
Results may differ from the reference program's by a relative error of at most 0.012.
The reference program's roundings to bfloat16 on the way count: a program that leaves them out, or rounds other values in their place, can miss the bound.
Values may be sent and summed in bfloat16 or wider, within the bound.
A program may use at most 192 MiB of HBM per device.

```python
import math
import jax
import jax.numpy as jnp
from jax import lax

D = 2048
HEADS = 32
HEAD_DIM = 64
ROT = 32
FF = 8192
TOK_DEV = 256
SEQ_LEN = 1024
SEQS = 8
TOKENS = 8192


def draw_segments(key, part):
    key = jax.random.fold_in(key, 11)
    side_key, early_key, late_key = jax.random.split(key, 3)
    side = jax.random.randint(side_key, (SEQS, 1), 0, 2)
    early = jax.random.randint(early_key, (SEQS, 1), SEQ_LEN // 5, TOK_DEV)
    late = jax.random.randint(late_key, (SEQS, 1), SEQ_LEN - TOK_DEV + 1, SEQ_LEN - SEQ_LEN // 5 + 1)
    boundary = side * early + (1 - side) * late
    places = jnp.arange(SEQ_LEN, dtype=jnp.int32)[None, :]
    return (places >= boundary).astype(jnp.int32)


def strengthened(result, own_key, source, target, shards_of, factor):
    owner, partner = [(jnp.arange(result.shape[dim]) // (result.shape[dim] // shards_of)).reshape([-1 if axis == dim else 1 for axis in range(result.ndim)]) for dim in (source, target)]
    chosen = jax.random.permutation(own_key, shards_of)[partner]
    strong = (owner == chosen) | (owner == (partner + shards_of // 2) % shards_of)
    return jnp.where(strong, factor * result, result)


def block_scale(key, dims, shards, least, largest):
    level = 1.0
    for dim, shards_of in shards:
        draws = jax.random.uniform(jax.random.fold_in(jax.random.fold_in(key, 6), dim), (shards_of,), jnp.float32, least / len(shards), largest / len(shards))
        level = level * jnp.repeat(jnp.exp(draws), dims[dim] // shards_of).reshape((-1,) + (1,) * (len(dims) - 1 - dim))
    return level


def bell_draw(rng, extent, deviation, most, cuts=(), held_as=jnp.bfloat16):
    array = jax.random.normal(rng, extent, jnp.float32) * deviation
    if len(cuts) > 0:
        array = block_scale(rng, extent, cuts, -0.22, 0.18) * array
    return jnp.clip(array, min=-most, max=most).astype(held_as)


def heavy_noise(rng, extent, width, limit, cuts, heavy, held_as=jnp.bfloat16):
    drawn = width * jax.random.normal(rng, extent, jnp.float32)
    if cuts:
        drawn = drawn * block_scale(rng, extent, cuts, -0.22, 0.18)
    return jnp.clip(strengthened(drawn, jax.random.fold_in(rng, 3), *heavy), -limit, limit).astype(held_as)


def setup_inputs(seed: int = 0) -> dict:
    key_list = jax.random.split(jax.random.key(seed), 14)
    return {
        "inputs": bell_draw(key_list[0], (TOKENS, D), 1.0, 6.0, ((0, 32),)),
        "segments": draw_segments(jax.random.fold_in(key_list[13], 71), 0),
        "ln_gain": jnp.clip(1.0 + 0.18 * jax.random.normal(key_list[2], (D,), jnp.float32), 0.099609375, 1.8984375).astype(jnp.bfloat16),
        "ln_bias": bell_draw(key_list[3], (D,), 0.3, 4.0),
        "w_qkv": bell_draw(key_list[4], (3, D, D), (D // 2) ** -0.5, 0.1875, ((1, 8), (2, 4))),
        "b_qkv": bell_draw(key_list[5], (3, D), 0.5, 6.0, ((1, 4),)),
        "w_out": bell_draw(key_list[6], (D, D), (D // 16) ** -0.5, 0.5, ((0, 4), (1, 8))),
        "b_out": bell_draw(key_list[7], (D,), 0.3, 4.0),
        "w_fc1": bell_draw(key_list[8], (D, FF), D ** -0.5, 0.125, ((0, 8), (1, 4))),
        "b_fc1": bell_draw(key_list[9], (FF,), 0.5, 6.0, ((0, 4),)),
        "w_fc2": bell_draw(key_list[10], (FF, D), FF ** -0.5, 0.0625, ((0, 4), (1, 8))),
        "b_fc2": bell_draw(key_list[11], (D,), 0.3, 4.0),
        "cotangent": heavy_noise(key_list[12], (TOKENS, D), 1.0, 6.0, ((0, 32),), (0, 1, 32, 2.75)),
    }


@jax.custom_vjp
def low(v):
    return lax.optimization_barrier(v.astype(jnp.bfloat16)).astype(jnp.float32)

@jax.custom_vjp
def low_back(v):
    return v

def low_keep(v):
    return (low(v), None)

def low_pass(kept, grad):
    return (grad,)

def back_keep(v):
    return (v, None)

def back_low(kept, grad):
    return (low(grad),)
low.defvjp(low_keep, low_pass)
low_back.defvjp(back_keep, back_low)
highest = lax.Precision.HIGHEST
norm_epsilon = 1e-05
masked_score = -1e+30

def gelu_tanh(values):
    return 0.5 * values * (1.0 + jnp.tanh(0.7978845608028654 * (values + 0.044715 * values * values * values)))

def layer_norm(tokens_in, gain, offset):
    centre = lax.optimization_barrier(jnp.mean(tokens_in, axis=-1, keepdims=True))
    centred = tokens_in - centre
    spread = lax.optimization_barrier(jnp.mean(centred * centred, axis=-1, keepdims=True))
    return centred * lax.rsqrt(spread + norm_epsilon) * gain + offset

def doc_positions(segment_row):
    places = jnp.arange(segment_row.shape[0], dtype=jnp.int32)
    opened = jnp.concatenate([jnp.ones((1,), dtype=jnp.bool_), segment_row[1:] != segment_row[:-1]])
    opening = lax.cummax(jnp.where(opened, places, jnp.zeros_like(places)), axis=0)
    return places - opening

def rotary_tables(segment_row):
    frequency = jnp.exp(jnp.arange(0, ROT, 2, dtype=jnp.float32) * (-math.log(10000.0) / ROT))
    angles = doc_positions(segment_row).astype(jnp.float32)[:, None] * frequency[None, :]
    angles = jnp.concatenate([angles, angles], axis=-1)[:, None, :]
    return (jnp.cos(angles), jnp.sin(angles))

def rotate(heads_data, cosine, sine_part):
    turned = heads_data[..., :ROT]
    half_rot = ROT // 2
    swapped = jnp.concatenate([-turned[..., half_rot:], turned[..., :half_rot]], axis=-1)
    return jnp.concatenate([turned * cosine + swapped * sine_part, heads_data[..., ROT:]], axis=-1)

def allowed_pairs(segment_row, first_row, row_count):
    places = jnp.arange(segment_row.shape[0], dtype=jnp.int32)
    row_places = places[first_row:first_row + row_count]
    row_segments = segment_row[first_row:first_row + row_count]
    return (row_places[:, None] >= places[None, :]) & (row_segments[:, None] == segment_row[None, :])

def sequence_forward(tokens_in, segment_row, weights):
    ln_gain, ln_bias, w_qkv, b_qkv, w_out, b_out, w_fc1, b_fc1, w_fc2, b_fc2 = weights
    length = tokens_in.shape[0]
    normed = low(layer_norm(tokens_in, ln_gain, ln_bias))
    projected = [low_back(jnp.dot(normed, w_qkv[which_one], precision=highest) + b_qkv[which_one]) for which_one in range(3)]
    shaped = [member.reshape(length, HEADS, HEAD_DIM) for member in projected]
    cosine, sine_part = rotary_tables(segment_row)
    queries = low(rotate(shaped[0], cosine, sine_part))
    key_heads = low(rotate(shaped[1], cosine, sine_part))
    values = low(shaped[2])
    scores = low_back(jnp.einsum('qhd,khd->hqk', queries, key_heads, precision=highest) * HEAD_DIM ** (-0.5))
    allowed = allowed_pairs(segment_row, 0, length)
    weights_soft = jax.nn.softmax(jnp.where(allowed[None], scores, masked_score), axis=-1)
    mixed_heads = jnp.einsum('hqk,khd->qhd', low(weights_soft), values, precision=highest).reshape(length, D)
    mixed_heads = low(low_back(mixed_heads))
    hidden = low_back(jnp.dot(normed, w_fc1, precision=highest) + b_fc1)
    active = low(gelu_tanh(hidden))
    branches = jnp.dot(mixed_heads, w_out, precision=highest) + jnp.dot(active, w_fc2, precision=highest)
    return tokens_in + branches + b_out + b_fc2

def reference(inputs, segments, ln_gain, ln_bias, w_qkv, b_qkv, w_out, b_out, w_fc1, b_fc1, w_fc2, b_fc2, cotangent):
    params = tuple((member.astype(jnp.float32) for member in (ln_gain, ln_bias, w_qkv, b_qkv, w_out, b_out, w_fc1, b_fc1, w_fc2, b_fc2)))
    tokens_all = inputs.astype(jnp.float32).reshape(SEQS, SEQ_LEN, D)
    grad_given = cotangent.astype(jnp.float32).reshape(SEQS, SEQ_LEN, D)

    def forward(tokens_seq, weights):
        per_sequence = jax.checkpoint(lambda tokens_one, segment_row: sequence_forward(tokens_one, segment_row, weights))

        def advance(carried, element):
            return (carried, per_sequence(element[0], element[1]))
        _, produced = lax.scan(advance, jnp.zeros((), jnp.float32), (tokens_seq, segments))
        return produced
    produced, pullback = jax.vjp(forward, tokens_all, params)
    grad_tokens, grad_params = pullback(grad_given)
    return (produced.reshape(TOKENS, D).astype(jnp.bfloat16), grad_tokens.reshape(TOKENS, D), grad_params[0], grad_params[1], grad_params[2], grad_params[3], grad_params[4], grad_params[5], grad_params[6], grad_params[7], grad_params[8], grad_params[9])
```

```python
import functools
import math

import jax
import jax.numpy as jnp
from jax import lax
from jax.experimental import pallas as pl
from jax.experimental.pallas import tpu as pltpu
from jax.sharding import PartitionSpec as P

D = 2048
HEAD_DIM = 64
ROT = 32
FF = 8192
MIB = 1 << 20

wide = jnp.float32
narrow = jnp.bfloat16
norm_epsilon = 1e-05
masked_score = -1e30


def gelu_tanh(values):
    return (
        0.5
        * values
        * (1.0 + jnp.tanh(0.7978845608028654 * (values + 0.044715 * values * values * values)))
    )


def layer_norm(tokens_in, gain, offset):
    centre = jnp.mean(tokens_in, axis=-1, keepdims=True)
    centred = tokens_in - centre
    spread = jnp.mean(centred * centred, axis=-1, keepdims=True)
    return centred * lax.rsqrt(spread + norm_epsilon) * gain + offset


def openings(segment_rows):
    places = jnp.broadcast_to(
        jnp.arange(segment_rows.shape[1], dtype=jnp.int32)[None], segment_rows.shape
    )
    opened = jnp.concatenate(
        [
            jnp.ones((segment_rows.shape[0], 1), dtype=jnp.bool_),
            segment_rows[:, 1:] != segment_rows[:, :-1],
        ],
        axis=1,
    )
    return lax.cummax(jnp.where(opened, places, jnp.zeros_like(places)), axis=1)


def rotary_tables(opening):
    length = opening.shape[1]
    places = jnp.arange(length, dtype=jnp.int32)[None]
    frequency = jnp.exp(jnp.arange(0, ROT, 2, dtype=jnp.float32) * (-math.log(10000.0) / ROT))
    angles = (places - opening).astype(jnp.float32)[:, :, None] * frequency
    cosine, sine = jnp.cos(angles), jnp.sin(angles)
    ones = jnp.ones(angles.shape[:2] + (HEAD_DIM - ROT,), wide)
    cos_head = jnp.concatenate([cosine, cosine, ones], axis=-1)
    sin_head = jnp.concatenate([-sine, sine, 0.0 * ones], axis=-1)
    return (
        jnp.concatenate([cos_head, cos_head], axis=-1),
        jnp.concatenate([sin_head, sin_head], axis=-1),
    )


def nt(a, b):
    return lax.dot_general(a, b, (((1,), (1,)), ((), ())), preferred_element_type=wide)


def nn(a, b):
    return lax.dot_general(a, b, (((1,), (0,)), ((), ())), preferred_element_type=wide)


def tn(a, b):
    return lax.dot_general(a, b, (((0,), (0,)), ((), ())), preferred_element_type=wide)


def attention_kernel(
    rows,
    open_ref,
    cos_ref,
    sin_ref,
    q_ref,
    k_ref,
    v_ref,
    do_ref,
    attn_ref,
    gq_ref,
    gk_ref,
    gv_ref,
    kb_ref,
    vb_ref,
    dk_ref,
    dv_ref,
):
    length = q_ref.shape[0]
    lanes = 2 * HEAD_DIM
    place = lax.broadcasted_iota(jnp.int32, (1, lanes), 1)
    low_half = (place % HEAD_DIM) < (ROT // 2)
    scale = HEAD_DIM**-0.5

    def partner(u):
        return jnp.where(
            low_half, pltpu.roll(u, lanes - ROT // 2, 1), pltpu.roll(u, ROT // 2, 1)
        )

    def turn(u, cosine, sine):
        return u * cosine + partner(u) * sine

    def turn_back(u, cosine, sine):
        return u * cosine - partner(u) * sine

    kb_ref[...] = turn(k_ref[...], cos_ref[...], sin_ref[...]).astype(narrow)
    vb_ref[...] = v_ref[...].astype(narrow)
    dk_ref[...] = jnp.zeros_like(dk_ref)
    dv_ref[...] = jnp.zeros_like(dv_ref)
    for first in range(0, length, rows):
        seen = first + rows
        here = slice(first, seen)
        cosine, sine = cos_ref[here], sin_ref[here]
        q_both = (turn(q_ref[here], cosine, sine).astype(narrow) * scale).astype(narrow)
        row_place = first + lax.broadcasted_iota(jnp.int32, (rows, seen), 0)
        key_place = lax.broadcasted_iota(jnp.int32, (rows, seen), 1)
        allowed = (key_place <= row_place) & (key_place >= open_ref[here])
        attn_parts, dq_parts, dk_parts, dv_parts = [], [], [], []
        for head in range(2):
            cols = slice(head * HEAD_DIM, (head + 1) * HEAD_DIM)
            q = q_both[:, cols]
            k, v = kb_ref[0:seen, cols], vb_ref[0:seen, cols]
            do = do_ref[here, cols]
            scores = jnp.where(allowed, nt(q, k), masked_score)
            largest = jnp.max(scores, axis=-1, keepdims=True)
            exponent = jnp.exp(scores - largest)
            probs = exponent * (1.0 / jnp.sum(exponent, axis=-1, keepdims=True))
            probs_low = probs.astype(narrow)
            attn_parts.append(nn(probs_low, v))
            grad_probs = nt(do, v)
            inner = jnp.sum(probs * grad_probs, axis=-1, keepdims=True)
            grad_scores = (probs * (grad_probs - inner)).astype(narrow)
            dq_parts.append(nn(grad_scores, k))
            dk_parts.append(tn(grad_scores, q))
            dv_parts.append(tn(probs_low, do))
        attn_ref[here] = jnp.concatenate(attn_parts, axis=1).astype(narrow)
        dq = jnp.concatenate(dq_parts, axis=1) * scale
        gq_ref[here] = turn_back(dq, cosine, sine).astype(narrow)
        dk_ref[0:seen] += jnp.concatenate(dk_parts, axis=1)
        dv_ref[0:seen] += jnp.concatenate(dv_parts, axis=1)
    gk_ref[...] = turn_back(dk_ref[...], cos_ref[...], sin_ref[...]).astype(narrow)
    gv_ref[...] = dv_ref[...].astype(narrow)


def attention(opening, cosine, sine, projected, grad_attn, length):
    tokens, width = grad_attn.shape
    lanes = 2 * HEAD_DIM
    pairs = width // lanes
    rows = min(256, length)
    col = pl.BlockSpec((length, 1), lambda s, h: (s, 0))
    table = pl.BlockSpec((length, lanes), lambda s, h: (s, 0))
    block = pl.BlockSpec((length, lanes), lambda s, h: (s, h))
    k_block = pl.BlockSpec((length, lanes), lambda s, h: (s, pairs + h))
    v_block = pl.BlockSpec((length, lanes), lambda s, h: (s, 2 * pairs + h))
    out = jax.ShapeDtypeStruct((tokens, width), narrow)
    return pl.pallas_call(
        functools.partial(attention_kernel, rows),
        grid=(tokens // length, pairs),
        in_specs=[col, table, table, block, k_block, v_block, block],
        out_specs=[block] * 4,
        out_shape=[out] * 4,
        scratch_shapes=[
            pltpu.VMEM((length, lanes), narrow),
            pltpu.VMEM((length, lanes), narrow),
            pltpu.VMEM((length, lanes), wide),
            pltpu.VMEM((length, lanes), wide),
        ],
        compiler_params=pltpu.CompilerParams(vmem_limit_bytes=48 * MIB),
        cost_estimate=pl.CostEstimate(
            flops=tokens * length * width * 12, bytes_accessed=tokens * width * 32, transcendentals=0
        ),
        name="attention",
    )(opening.reshape(tokens, 1), cosine.reshape(tokens, lanes), sine.reshape(tokens, lanes),
      projected, projected, projected, grad_attn)


def after(value, *earlier):
    return lax.optimization_barrier((value,) + earlier)[0]


def solution(mesh):
    nf = mesh.shape["fsdp"]
    nt_axis = mesh.shape["tp"]
    planes = nf // 2
    swap_f = [(f, f ^ 1) for f in range(nf)]
    up = [(f, f + 2) for f in range(nf - 2)]
    down = [(f + 2, f) for f in range(nf - 2)]
    swap_core = [(t, t ^ 1) for t in range(nt_axis)]
    swap_chip = [(t, t ^ 2) for t in range(nt_axis)]

    def send_x(v):
        return lax.ppermute(v, "fsdp", swap_f)

    def send_y(v):
        return lax.ppermute(v, "tp", swap_chip)

    def send_core(v):
        return lax.ppermute(v, "tp", swap_core)

    def local(
        inputs,
        segments,
        ln_gain,
        ln_bias,
        w_qkv,
        b_qkv,
        w_out,
        b_out,
        w_fc1,
        b_fc1,
        w_fc2,
        b_fc2,
        cotangent,
    ):
        f_place = lax.axis_index("fsdp")
        t_place = lax.axis_index("tp")
        plane, side = f_place // 2, f_place % 2
        chip, core = t_place // 2, t_place % 2
        length = segments.shape[1]
        mine = inputs.shape[0]
        rows = w_fc1.shape[0]
        group = 2 * rows

        def relative(v):
            blocks = v.reshape(v.shape[:-1] + (planes, group))
            flipped = jnp.flip(blocks, axis=-2)
            twice = jnp.concatenate([flipped, flipped], axis=-2)
            cut = lax.dynamic_slice_in_dim(twice, planes - 1 - plane, planes, axis=twice.ndim - 2)
            return cut.reshape(v.shape)

        def pick(v, index, axis=0):
            return lax.dynamic_index_in_dim(v, index, axis, keepdims=False)

        half_qkv, half_ff = w_qkv.shape[2] // 2, w_fc1.shape[1] // 2
        qkv_halves = w_qkv.transpose(1, 0, 2).reshape(rows, 3, 2, half_qkv).transpose(2, 0, 1, 3)
        qkv_halves = qkv_halves.reshape(2, rows, 3 * half_qkv)
        out_halves = w_out.T.reshape(rows, 2, half_qkv).transpose(1, 0, 2)
        qo_halves = jnp.concatenate([qkv_halves, out_halves], axis=2)
        fc1_halves = w_fc1.reshape(rows, 2, half_ff).transpose(1, 0, 2)
        fc2_halves = w_fc2.T.reshape(rows, 2, half_ff).transpose(1, 0, 2)
        quarter = half_ff // 2

        def both_rows(kept, came):
            return jnp.where(
                side == 0, jnp.concatenate([kept, came], 0), jnp.concatenate([came, kept], 0)
            )

        token = [inputs]

        def gather_planes(halves):
            kept, sent = pick(halves, side), pick(halves, 1 - side)
            own = both_rows(kept, send_x(sent))
            ups, downs = [own], [own]
            for step in range(planes - 1):
                to_up, to_down, _ = lax.optimization_barrier((ups[-1], downs[-1], token[0]))
                ups.append(lax.ppermute(to_up, "fsdp", up))
                downs.append(lax.ppermute(to_down, "fsdp", down))
                token[0] = (ups[-1], downs[-1])
            blocks = [own] + [ups[d] + downs[planes - d] for d in range(1, planes)]
            return jnp.concatenate(blocks, axis=0)

        def scatter_planes(grads):
            low = grads.astype(narrow).reshape(planes, group, grads.shape[1])
            going_up = going_down = None
            for step in range(1, planes):
                up_part, down_part = low[step], low[planes - step]
                if going_up is not None:
                    up_part = (up_part.astype(wide) + going_up.astype(wide)).astype(narrow)
                    down_part = (down_part.astype(wide) + going_down.astype(wide)).astype(narrow)
                going_up = lax.ppermute(up_part, "fsdp", up)
                going_down = lax.ppermute(down_part, "fsdp", down)
            total = low[0].astype(wide)
            if going_up is not None:
                total = total + going_up.astype(wide) + going_down.astype(wide)
            parts = total.reshape(2, rows, grads.shape[1])
            came = send_x(pick(parts, 1 - side).astype(narrow)).astype(wide)
            kept = pick(parts, side)
            return jnp.where(side == 0, jnp.stack([kept, came]), jnp.stack([came, kept]))

        def gather_tokens(own, x_last):
            over_y = send_y(own)
            over_x = send_x(own)
            over_both = send_x(over_y) if x_last else send_y(over_x)
            spot = jnp.zeros((2, 2) + own.shape, own.dtype)
            for a, b, v in (
                (side, chip, own),
                (side, 1 - chip, over_y),
                (1 - side, chip, over_x),
                (1 - side, 1 - chip, over_both),
            ):
                spot = lax.dynamic_update_slice(spot, v[None, None], (a, b, 0, 0))
            other = send_core(spot)
            pair = jnp.where(
                core == 0, jnp.stack([spot, other], axis=2), jnp.stack([other, spot], axis=2)
            )
            return pair.reshape(8 * own.shape[0], own.shape[1])

        def scatter_tokens(total):
            parts = total.reshape(2, 2, 2, mine, D)
            came = send_core(pick(parts, 1 - core, 2).astype(narrow))
            summed = pick(parts, core, 2).astype(wide) + came.astype(wide)
            halves = []
            for number, columns in enumerate((summed[..., : D // 2], summed[..., D // 2 :])):
                if number == 0:
                    came = send_x(pick(columns, 1 - side, 0).astype(narrow))
                    part = pick(columns, side, 0) + came.astype(wide)
                    came = send_y(pick(part, 1 - chip, 0).astype(narrow))
                    part = pick(part, chip, 0) + came.astype(wide)
                else:
                    came = send_y(pick(columns, 1 - chip, 1).astype(narrow))
                    part = pick(columns, chip, 1) + came.astype(wide)
                    came = send_x(pick(part, 1 - side, 0).astype(narrow))
                    part = pick(part, side, 0) + came.astype(wide)
                halves.append(part)
            return relative(jnp.concatenate(halves, axis=1))

        def reduce_all(v):
            for axis, size in (("tp", nt_axis), ("fsdp", nf)):
                bit = 1
                while bit < size:
                    v = v + lax.ppermute(v, axis, [(i, i ^ bit) for i in range(size)])
                    bit *= 2
            return v

        tokens_in = inputs.astype(wide)
        normed_local, norm_back = jax.vjp(
            layer_norm, tokens_in, ln_gain.astype(wide), ln_bias.astype(wide)
        )
        normed = gather_tokens(relative(normed_local.astype(narrow)), True)
        grad_rows = gather_tokens(relative(cotangent), False)
        other_segments = send_x(segments)
        both_segments = jnp.where(
            side == 0,
            jnp.concatenate([segments, other_segments], 0),
            jnp.concatenate([other_segments, segments], 0),
        )
        opening = openings(both_segments)
        cosine, sine = rotary_tables(opening)

        full_qo = gather_planes(qo_halves)
        full_fc1a = gather_planes(fc1_halves[:, :, :quarter])
        full_fc2a = gather_planes(fc2_halves[:, :, :quarter])
        full_fc1b = gather_planes(fc1_halves[:, :, quarter:])
        full_fc2b = gather_planes(fc2_halves[:, :, quarter:])

        full_qkv, full_out = full_qo[:, : 3 * half_qkv], full_qo[:, 3 * half_qkv :]
        bias_qkv = lax.dynamic_slice_in_dim(b_qkv, side * half_qkv, half_qkv, axis=1)
        bias_fc1 = lax.dynamic_slice_in_dim(b_fc1, side * half_ff, half_ff, axis=0)

        projected = nn(normed, full_qkv) + bias_qkv.astype(wide).reshape(1, 3 * half_qkv)
        grad_mixed = nn(grad_rows, full_out).astype(narrow)
        mixed, grad_q, grad_k, grad_v = attention(
            opening, cosine, sine, projected, grad_mixed, length
        )
        grad_projected = jnp.concatenate([grad_q, grad_k, grad_v], axis=1)
        grad_qo = jnp.concatenate([tn(normed, grad_projected), tn(grad_rows, mixed)], axis=1)
        sum_qo = scatter_planes(grad_qo)

        sums_fc1, sums_fc2, hidden_sums = [], [], []
        branches = nt(mixed, full_out)
        grad_normed = nt(grad_projected, full_qkv)
        for number, (full_fc1, full_fc2) in enumerate(
            ((full_fc1a, full_fc2a), (full_fc1b, full_fc2b))
        ):
            bias = bias_fc1[number * quarter : (number + 1) * quarter].astype(wide)
            hidden = nn(normed, full_fc1) + bias
            active, gelu_back = jax.vjp(gelu_tanh, hidden)
            active_low = active.astype(narrow)
            sums_fc2.append(scatter_planes(tn(grad_rows, active_low)))
            grad_hidden = gelu_back(nn(grad_rows, full_fc2))[0].astype(narrow)
            sums_fc1.append(scatter_planes(tn(normed, grad_hidden)))
            hidden_sums.append(jnp.sum(grad_hidden.astype(wide), axis=0))
            branches = branches + nt(active_low, full_fc2)
            grad_normed = grad_normed + nt(grad_hidden, full_fc1)

        branch_local = scatter_tokens(branches)
        outputs = (tokens_in + branch_local + b_out.astype(wide) + b_fc2.astype(wide)).astype(narrow)
        grad_tokens, grad_gain, grad_offset = norm_back(scatter_tokens(grad_normed))
        grad_tokens = grad_tokens + cotangent.astype(wide)

        grad_w_qkv = sum_qo[:, :, : 3 * half_qkv].reshape(2, rows, 3, half_qkv)
        grad_w_qkv = grad_w_qkv.transpose(2, 1, 0, 3).reshape(3, rows, 2 * half_qkv)
        grad_w_out = sum_qo[:, :, 3 * half_qkv :].transpose(0, 2, 1).reshape(2 * half_qkv, rows)

        def joined(a, b):
            both = jnp.concatenate([a, b], axis=2)
            return both.transpose(1, 0, 2).reshape(rows, 2 * half_ff)

        grad_w_fc1 = joined(*sums_fc1)
        grad_w_fc2 = joined(*sums_fc2).T

        anchor = jnp.zeros((), jnp.int32)
        bias_qkv_full = lax.dynamic_update_slice(
            jnp.zeros((3, D), wide),
            jnp.sum(grad_projected.astype(wide), axis=0).reshape(3, half_qkv),
            (anchor, (2 * t_place + side) * half_qkv),
        )
        bias_fc1_full = lax.dynamic_update_slice(
            jnp.zeros((FF,), wide),
            jnp.concatenate(hidden_sums),
            ((2 * t_place + side) * half_ff,),
        )
        cotangent_sum = jnp.sum(cotangent.astype(wide), axis=0)
        small = reduce_all(
            jnp.concatenate(
                [bias_qkv_full.reshape(-1), bias_fc1_full, grad_gain, grad_offset, cotangent_sum]
            ).reshape(-1, 128)
        ).reshape(-1)
        total_qkv = small[: 3 * D].reshape(3, D)
        total_fc1 = small[3 * D : 3 * D + FF]
        total_gain, total_offset, total_out = small[3 * D + FF :].reshape(3, D)
        return (
            outputs,
            grad_tokens,
            total_gain,
            total_offset,
            grad_w_qkv,
            total_qkv,
            grad_w_out,
            total_out,
            grad_w_fc1,
            total_fc1,
            grad_w_fc2,
            total_out,
        )

    return jax.shard_map(
        local,
        mesh=mesh,
        in_specs=(
            P(("fsdp", "tp"), None),
            P("fsdp", None),
            P(),
            P(),
            P(None, "fsdp", "tp"),
            P(None, "tp"),
            P("tp", "fsdp"),
            P(),
            P("fsdp", "tp"),
            P("tp"),
            P("tp", "fsdp"),
            P(),
            P(("fsdp", "tp"), None),
        ),
        out_specs=(
            P(("fsdp", "tp"), None),
            P(("fsdp", "tp"), None),
            P(),
            P(),
            P(None, "fsdp", "tp"),
            P(),
            P("tp", "fsdp"),
            P(),
            P("fsdp", "tp"),
            P(),
            P("tp", "fsdp"),
            P(),
        ),
        check_vma=False,
    )
```

```python
import functools
import math

import jax
import jax.numpy as jnp
from jax import lax
from jax.experimental import pallas as pl
from jax.experimental.pallas import tpu as pltpu
from jax.sharding import PartitionSpec as P

D = 2048
HEAD_DIM = 64
ROT = 32
FF = 8192
MIB = 1 << 20

wide = jnp.float32
narrow = jnp.bfloat16
norm_epsilon = 1e-05
masked_score = -1e30


def gelu_tanh(values):
    return (
        0.5
        * values
        * (1.0 + jnp.tanh(0.7978845608028654 * (values + 0.044715 * values * values * values)))
    )


def layer_norm(tokens_in, gain, offset):
    centre = jnp.mean(tokens_in, axis=-1, keepdims=True)
    centred = tokens_in - centre
    spread = jnp.mean(centred * centred, axis=-1, keepdims=True)
    return centred * lax.rsqrt(spread + norm_epsilon) * gain + offset


def openings(segment_rows):
    places = jnp.broadcast_to(
        jnp.arange(segment_rows.shape[1], dtype=jnp.int32)[None], segment_rows.shape
    )
    opened = jnp.concatenate(
        [
            jnp.ones((segment_rows.shape[0], 1), dtype=jnp.bool_),
            segment_rows[:, 1:] != segment_rows[:, :-1],
        ],
        axis=1,
    )
    return lax.cummax(jnp.where(opened, places, jnp.zeros_like(places)), axis=1)


def rotary_tables(opening):
    length = opening.shape[1]
    places = jnp.arange(length, dtype=jnp.int32)[None]
    frequency = jnp.exp(jnp.arange(0, ROT, 2, dtype=jnp.float32) * (-math.log(10000.0) / ROT))
    angles = (places - opening).astype(jnp.float32)[:, :, None] * frequency
    cosine, sine = jnp.cos(angles), jnp.sin(angles)
    ones = jnp.ones(angles.shape[:2] + (HEAD_DIM - ROT,), wide)
    cos_head = jnp.concatenate([cosine, cosine, ones], axis=-1)
    sin_head = jnp.concatenate([-sine, sine, 0.0 * ones], axis=-1)
    return (
        jnp.concatenate([cos_head, cos_head], axis=-1),
        jnp.concatenate([sin_head, sin_head], axis=-1),
    )


def nt(a, b):
    return lax.dot_general(a, b, (((1,), (1,)), ((), ())), preferred_element_type=wide)


def nn(a, b):
    return lax.dot_general(a, b, (((1,), (0,)), ((), ())), preferred_element_type=wide)


def tn(a, b):
    return lax.dot_general(a, b, (((0,), (0,)), ((), ())), preferred_element_type=wide)


def attention_kernel(
    rows,
    open_ref,
    cos_ref,
    sin_ref,
    q_ref,
    k_ref,
    v_ref,
    do_ref,
    attn_ref,
    gq_ref,
    gk_ref,
    gv_ref,
    kb_ref,
    vb_ref,
    dk_ref,
    dv_ref,
):
    length = q_ref.shape[0]
    lanes = 2 * HEAD_DIM
    place = lax.broadcasted_iota(jnp.int32, (1, lanes), 1)
    low_half = (place % HEAD_DIM) < (ROT // 2)
    scale = HEAD_DIM**-0.5

    def partner(u):
        return jnp.where(
            low_half, pltpu.roll(u, lanes - ROT // 2, 1), pltpu.roll(u, ROT // 2, 1)
        )

    def turn(u, cosine, sine):
        return u * cosine + partner(u) * sine

    def turn_back(u, cosine, sine):
        return u * cosine - partner(u) * sine

    kb_ref[...] = turn(k_ref[...], cos_ref[...], sin_ref[...]).astype(narrow)
    vb_ref[...] = v_ref[...].astype(narrow)
    dk_ref[...] = jnp.zeros_like(dk_ref)
    dv_ref[...] = jnp.zeros_like(dv_ref)
    for first in range(0, length, rows):
        seen = first + rows
        here = slice(first, seen)
        cosine, sine = cos_ref[here], sin_ref[here]
        q_both = (turn(q_ref[here], cosine, sine).astype(narrow) * scale).astype(narrow)
        row_place = first + lax.broadcasted_iota(jnp.int32, (rows, seen), 0)
        key_place = lax.broadcasted_iota(jnp.int32, (rows, seen), 1)
        allowed = (key_place <= row_place) & (key_place >= open_ref[here])
        attn_parts, dq_parts, dk_parts, dv_parts = [], [], [], []
        for head in range(2):
            cols = slice(head * HEAD_DIM, (head + 1) * HEAD_DIM)
            q = q_both[:, cols]
            k, v = kb_ref[0:seen, cols], vb_ref[0:seen, cols]
            do = do_ref[here, cols]
            scores = jnp.where(allowed, nt(q, k), masked_score)
            largest = jnp.max(scores, axis=-1, keepdims=True)
            exponent = jnp.exp(scores - largest)
            probs = exponent * (1.0 / jnp.sum(exponent, axis=-1, keepdims=True))
            probs_low = probs.astype(narrow)
            attn_parts.append(nn(probs_low, v))
            grad_probs = nt(do, v)
            inner = jnp.sum(probs * grad_probs, axis=-1, keepdims=True)
            grad_scores = (probs * (grad_probs - inner)).astype(narrow)
            dq_parts.append(nn(grad_scores, k))
            dk_parts.append(tn(grad_scores, q))
            dv_parts.append(tn(probs_low, do))
        attn_ref[here] = jnp.concatenate(attn_parts, axis=1).astype(narrow)
        dq = jnp.concatenate(dq_parts, axis=1) * scale
        gq_ref[here] = turn_back(dq, cosine, sine).astype(narrow)
        dk_ref[0:seen] += jnp.concatenate(dk_parts, axis=1)
        dv_ref[0:seen] += jnp.concatenate(dv_parts, axis=1)
    gk_ref[...] = turn_back(dk_ref[...], cos_ref[...], sin_ref[...]).astype(narrow)
    gv_ref[...] = dv_ref[...].astype(narrow)


def attention(opening, cosine, sine, projected, grad_attn, length):
    tokens, width = grad_attn.shape
    lanes = 2 * HEAD_DIM
    pairs = width // lanes
    rows = min(256, length)
    col = pl.BlockSpec((length, 1), lambda s, h: (s, 0))
    table = pl.BlockSpec((length, lanes), lambda s, h: (s, 0))
    block = pl.BlockSpec((length, lanes), lambda s, h: (s, h))
    k_block = pl.BlockSpec((length, lanes), lambda s, h: (s, pairs + h))
    v_block = pl.BlockSpec((length, lanes), lambda s, h: (s, 2 * pairs + h))
    out = jax.ShapeDtypeStruct((tokens, width), narrow)
    return pl.pallas_call(
        functools.partial(attention_kernel, rows),
        grid=(tokens // length, pairs),
        in_specs=[col, table, table, block, k_block, v_block, block],
        out_specs=[block] * 4,
        out_shape=[out] * 4,
        scratch_shapes=[
            pltpu.VMEM((length, lanes), narrow),
            pltpu.VMEM((length, lanes), narrow),
            pltpu.VMEM((length, lanes), wide),
            pltpu.VMEM((length, lanes), wide),
        ],
        compiler_params=pltpu.CompilerParams(vmem_limit_bytes=48 * MIB),
        cost_estimate=pl.CostEstimate(
            flops=tokens * length * width * 12, bytes_accessed=tokens * width * 32, transcendentals=0
        ),
        name="attention",
    )(opening.reshape(tokens, 1), cosine.reshape(tokens, lanes), sine.reshape(tokens, lanes),
      projected, projected, projected, grad_attn)


MESH = pl.DeviceIdType.MESH


def neighbours():
    f_place, t_place = lax.axis_index("fsdp"), lax.axis_index("tp")
    side, chip, core = f_place % 2, t_place // 2, t_place % 2
    over_x = {"fsdp": f_place + 1 - 2 * side, "tp": t_place}
    over_y = {"fsdp": f_place, "tp": t_place + 2 - 4 * chip}
    over_core = {"fsdp": f_place, "tp": t_place + 1 - 2 * core}
    return side, chip, core, over_x, over_y, over_core


def greet(*others):
    barrier = pltpu.get_barrier_semaphore()
    for other in others:
        pl.semaphore_signal(barrier, inc=1, device_id=other, device_id_type=MESH)
    pl.semaphore_wait(barrier, len(others))


class Copies:
    def __init__(self, send_sems, recv_sems):
        self.send_sems, self.recv_sems, self.count, self.started = send_sems, recv_sems, 0, []

    def remote(self, source, target, device):
        copy = pltpu.make_async_remote_copy(
            src_ref=source,
            dst_ref=target,
            send_sem=self.send_sems.at[self.count],
            recv_sem=self.recv_sems.at[self.count],
            device_id=device,
            device_id_type=MESH,
        )
        self.count += 1
        copy.start()
        self.started.append(copy)
        return copy

    def local(self, source, target):
        copy = pltpu.make_async_copy(source, target, self.send_sems.at[self.count])
        self.count += 1
        copy.start()
        return copy


def half(ref, which, width):
    return pl.ds(pl.multiple_of(which * width, 128), width)


def exchange_qo_kernel(qkv_ref, out_ref, block_ref, send_sems, recv_sems):
    side, _, _, over_x, _, _ = neighbours()
    width = out_ref.shape[1] // 2
    greet(over_x)
    copies = Copies(send_sems, recv_sems)
    kept = []
    for part in range(4):
        source = qkv_ref.at[part] if part < 3 else out_ref
        target = block_ref.at[side, :, pl.ds(part * width, width)]
        copies.remote(source.at[:, half(source, 1 - side, width)], target, over_x)
        kept.append(copies.local(source.at[:, half(source, side, width)], target))
    for copy in kept + copies.started:
        copy.wait()


def exchange_qo(w_qkv, w_out_rows):
    rows, columns = w_out_rows.shape
    return pl.pallas_call(
        exchange_qo_kernel,
        in_specs=[pl.BlockSpec(memory_space=pl.ANY)] * 2,
        out_specs=pl.BlockSpec(memory_space=pl.ANY),
        out_shape=jax.ShapeDtypeStruct((2, rows, 2 * columns), narrow),
        scratch_shapes=[pltpu.SemaphoreType.DMA((8,)), pltpu.SemaphoreType.DMA((8,))],
        compiler_params=pltpu.CompilerParams(collective_id=0, has_side_effects=True),
        name="exchange_qo",
    )(w_qkv, w_out_rows)


def gather_kernel(
    normed_ref, given_ref, fc1_ref, fc2_ref, normed_all, given_all, fc1_block, fc2_block, send_sems, recv_sems
):
    side, chip, core, over_x, over_y, over_core = neighbours()
    rows = normed_ref.shape[0]
    cut = rows // 2
    width = fc1_ref.shape[1] // 2
    greet(over_x, over_y, over_core)
    copies = Copies(send_sems, recv_sems)
    waits = []
    arrays = ((normed_ref, normed_all), (given_ref, given_all))
    first = []
    for own, whole in arrays:
        mine = whole.at[side, chip, core]
        first.append((copies.remote(own, mine, over_y), copies.remote(own, mine, over_x)))
        waits.append(copies.local(own, mine))
        copies.remote(own, mine, over_core)
    for weight, block in ((fc1_ref, fc1_block), (fc2_ref, fc2_block)):
        copies.remote(weight.at[:, half(weight, 1 - side, width)], block.at[side], over_x)
        waits.append(copies.local(weight.at[:, half(weight, side, width)], block.at[side]))
    corner = []
    for number, (_, whole) in enumerate(arrays):
        from_y, from_x = first[number]
        y_slot, x_slot = whole.at[side, 1 - chip, core], whole.at[1 - side, chip, core]
        from_y.wait_recv()
        if number == 0:
            part = y_slot.at[pl.ds(0, cut)]
            a = copies.remote(part, part, over_x)
        copies.remote(y_slot, y_slot, over_core)
        from_x.wait_recv()
        if number == 0:
            part = x_slot.at[pl.ds(cut, rows - cut)]
            b = copies.remote(part, part, over_y)
            corner.append((a, b))
        else:
            corner.append((copies.remote(x_slot, x_slot, over_y),))
        copies.remote(x_slot, x_slot, over_core)
    for number, (_, whole) in enumerate(arrays):
        for copy in corner[number]:
            copy.wait_recv()
        slot = whole.at[1 - side, 1 - chip, core]
        copies.remote(slot, slot, over_core)
    done = [copy for pair in first for copy in pair] + [copy for group in corner for copy in group]
    for copy in waits:
        copy.wait()
    for copy in copies.started:
        copy.wait_send()
        if not any(copy is other for other in done):
            copy.wait_recv()


def gather_tokens(normed, given, fc1, fc2_rows):
    mine, rows = normed.shape[0], fc1.shape[0]
    whole = jax.ShapeDtypeStruct((2, 2, 2, mine, D), narrow)
    block = jax.ShapeDtypeStruct((2, rows, fc1.shape[1] // 2), narrow)
    normed_all, given_all, fc1_block, fc2_block = pl.pallas_call(
        gather_kernel,
        in_specs=[pl.BlockSpec(memory_space=pl.ANY)] * 4,
        out_specs=[pl.BlockSpec(memory_space=pl.ANY)] * 4,
        out_shape=[whole, whole, block, block],
        scratch_shapes=[pltpu.SemaphoreType.DMA((24,)), pltpu.SemaphoreType.DMA((24,))],
        compiler_params=pltpu.CompilerParams(collective_id=1, has_side_effects=True),
        name="gather_tokens",
    )(normed, given, fc1, fc2_rows)
    return normed_all.reshape(8 * mine, D), given_all.reshape(8 * mine, D), fc1_block, fc2_block


def product_kernel(count, *refs):
    total = nt(refs[0][...], refs[count][...])
    for number in range(1, count):
        total += nt(refs[number][...], refs[count + number][...])
    refs[2 * count][...] = total.astype(narrow)


def sum_of_products(pairs):
    tokens = pairs[0][0].shape[0]
    block = min(256, tokens)
    left = [pl.BlockSpec((block, a.shape[1]), lambda i: (i, 0)) for a, _, _ in pairs]
    right = [
        pl.BlockSpec((w.shape[0], a.shape[1]), functools.partial(lambda c, i: (0, c), c))
        for a, w, c in pairs
    ]
    depth = sum(a.shape[1] for a, _, _ in pairs)
    return pl.pallas_call(
        functools.partial(product_kernel, len(pairs)),
        grid=(tokens // block,),
        in_specs=left + right,
        out_specs=pl.BlockSpec((block, D), lambda i: (i, 0)),
        out_shape=jax.ShapeDtypeStruct((tokens, D), narrow),
        compiler_params=pltpu.CompilerParams(vmem_limit_bytes=48 * MIB),
        cost_estimate=pl.CostEstimate(
            flops=2 * tokens * depth * D, bytes_accessed=2 * depth * (tokens + D), transcendentals=0
        ),
        name="sum_of_products",
    )(*[a for a, _, _ in pairs], *[w for _, w, _ in pairs])


def solution(mesh):
    nf = mesh.shape["fsdp"]
    nt_axis = mesh.shape["tp"]
    columns_of_planes = [list(range(side, nf, 2)) for side in range(2)]
    swap_f = [(f, f ^ 1) for f in range(nf)]
    swap_core = [(t, t ^ 1) for t in range(nt_axis)]
    swap_chip = [(t, t ^ 2) for t in range(nt_axis)]

    def send_x(v):
        return lax.ppermute(v, "fsdp", swap_f)

    def send_y(v):
        return lax.ppermute(v, "tp", swap_chip)

    def send_core(v):
        return lax.ppermute(v, "tp", swap_core)

    def gather_planes(block):
        block = block.reshape(block.shape[0] * block.shape[1], block.shape[2])
        return lax.all_gather(
            block, "fsdp", axis=0, tiled=True, axis_index_groups=columns_of_planes
        )

    def local(
        inputs,
        segments,
        ln_gain,
        ln_bias,
        w_qkv,
        b_qkv,
        w_out,
        b_out,
        w_fc1,
        b_fc1,
        w_fc2,
        b_fc2,
        cotangent,
    ):
        f_place = lax.axis_index("fsdp")
        t_place = lax.axis_index("tp")
        side = f_place % 2
        chip, core = t_place // 2, t_place % 2
        length = segments.shape[1]
        mine = inputs.shape[0]
        rows = w_fc1.shape[0]
        half_qkv, half_ff = w_qkv.shape[2] // 2, w_fc1.shape[1] // 2

        def pick(v, index, axis=0):
            return lax.dynamic_index_in_dim(v, index, axis, keepdims=False)

        def in_order(kept, came):
            return jnp.where(side == 0, jnp.stack([kept, came]), jnp.stack([came, kept]))

        def scatter_planes(grads):
            total = lax.psum_scatter(
                grads.astype(narrow),
                "fsdp",
                scatter_dimension=0,
                tiled=True,
                axis_index_groups=columns_of_planes,
            )
            parts = total.reshape(2, rows, grads.shape[1])
            came = send_x(pick(parts, 1 - side))
            return in_order(pick(parts, side), came).astype(wide)

        def scatter_tokens(total):
            parts = total.reshape(2, 2, 2, mine, D)
            came = send_core(pick(parts, 1 - core, 2).astype(narrow))
            summed = pick(parts, core, 2).astype(wide) + came.astype(wide)
            halves = []
            for number, columns in enumerate((summed[..., : D // 2], summed[..., D // 2 :])):
                if number == 0:
                    came = send_x(pick(columns, 1 - side, 0).astype(narrow))
                    part = pick(columns, side, 0) + came.astype(wide)
                    came = send_y(pick(part, 1 - chip, 0).astype(narrow))
                    part = pick(part, chip, 0) + came.astype(wide)
                else:
                    came = send_y(pick(columns, 1 - chip, 1).astype(narrow))
                    part = pick(columns, chip, 1) + came.astype(wide)
                    came = send_x(pick(part, 1 - side, 0).astype(narrow))
                    part = pick(part, side, 0) + came.astype(wide)
                halves.append(part)
            return jnp.concatenate(halves, axis=1)

        def reduce_all(v):
            for axis, size in (("tp", nt_axis), ("fsdp", nf)):
                bit = 1
                while bit < size:
                    v = v + lax.ppermute(v, axis, [(i, i ^ bit) for i in range(size)])
                    bit *= 2
            return v

        full_qo = gather_planes(exchange_qo(w_qkv, w_out.T))

        tokens_in = inputs.astype(wide)
        normed_local, norm_back = jax.vjp(
            layer_norm, tokens_in, ln_gain.astype(wide), ln_bias.astype(wide)
        )
        normed, grad_rows, fc1_block, fc2_block = gather_tokens(
            normed_local.astype(narrow), cotangent, w_fc1, w_fc2.T
        )
        full_fc1, full_fc2 = gather_planes(fc1_block), gather_planes(fc2_block)
        both_segments = in_order(segments[0], send_x(segments)[0])
        opening = openings(both_segments)
        cosine, sine = rotary_tables(opening)

        full_qkv, full_out = full_qo[:, : 3 * half_qkv], full_qo[:, 3 * half_qkv :]
        bias_qkv = lax.dynamic_slice_in_dim(b_qkv, side * half_qkv, half_qkv, axis=1)
        bias_fc1 = lax.dynamic_slice_in_dim(b_fc1, side * half_ff, half_ff, axis=0)

        projected = nn(normed, full_qkv) + bias_qkv.astype(wide).reshape(1, 3 * half_qkv)
        grad_mixed = nn(grad_rows, full_out).astype(narrow)
        mixed, grad_q, grad_k, grad_v = attention(
            opening, cosine, sine, projected, grad_mixed, length
        )
        grad_projected = jnp.concatenate([grad_q, grad_k, grad_v], axis=1)
        grad_qo = jnp.concatenate(
            [tn(normed, grad_projected).astype(narrow), tn(grad_rows, mixed).astype(narrow)], axis=1
        )
        sum_qo = scatter_planes(grad_qo)

        hidden = nn(normed, full_fc1) + bias_fc1.astype(wide)
        active, gelu_back = jax.vjp(gelu_tanh, hidden)
        active_low = active.astype(narrow)
        sum_fc2 = scatter_planes(tn(grad_rows, active_low))
        grad_hidden = gelu_back(nn(grad_rows, full_fc2))[0].astype(narrow)
        sum_fc1 = scatter_planes(tn(normed, grad_hidden))
        grad_normed = scatter_tokens(
            sum_of_products(
                [(grad_q, full_qo, 0), (grad_k, full_qo, 1), (grad_v, full_qo, 2), (grad_hidden, full_fc1, 0)]
            )
        )
        branch_local = scatter_tokens(
            sum_of_products([(mixed, full_qo, 3), (active_low, full_fc2, 0)])
        )
        outputs = (tokens_in + branch_local + b_out.astype(wide) + b_fc2.astype(wide)).astype(narrow)
        grad_tokens, grad_gain, grad_offset = norm_back(grad_normed)
        grad_tokens = grad_tokens + cotangent.astype(wide)

        grad_w_qkv = sum_qo[:, :, : 3 * half_qkv].reshape(2, rows, 3, half_qkv)
        grad_w_qkv = grad_w_qkv.transpose(2, 1, 0, 3).reshape(3, rows, 2 * half_qkv)
        grad_w_out = sum_qo[:, :, 3 * half_qkv :].transpose(0, 2, 1).reshape(2 * half_qkv, rows)
        grad_w_fc1 = sum_fc1.transpose(1, 0, 2).reshape(rows, 2 * half_ff)
        grad_w_fc2 = sum_fc2.transpose(0, 2, 1).reshape(2 * half_ff, rows)

        anchor = jnp.zeros((), jnp.int32)
        bias_qkv_full = lax.dynamic_update_slice(
            jnp.zeros((3, D), wide),
            jnp.sum(grad_projected.astype(wide), axis=0).reshape(3, half_qkv),
            (anchor, (2 * t_place + side) * half_qkv),
        )
        bias_fc1_full = lax.dynamic_update_slice(
            jnp.zeros((FF,), wide),
            jnp.sum(grad_hidden.astype(wide), axis=0),
            ((2 * t_place + side) * half_ff,),
        )
        cotangent_sum = jnp.sum(cotangent.astype(wide), axis=0)
        small = reduce_all(
            jnp.concatenate(
                [bias_qkv_full.reshape(-1), bias_fc1_full, grad_gain, grad_offset, cotangent_sum]
            ).reshape(-1, 128)
        ).reshape(-1)
        total_qkv = small[: 3 * D].reshape(3, D)
        total_fc1 = small[3 * D : 3 * D + FF]
        total_gain, total_offset, total_out = small[3 * D + FF :].reshape(3, D)
        return (
            outputs,
            grad_tokens,
            total_gain,
            total_offset,
            grad_w_qkv,
            total_qkv,
            grad_w_out,
            total_out,
            grad_w_fc1,
            total_fc1,
            grad_w_fc2,
            total_out,
        )

    return jax.shard_map(
        local,
        mesh=mesh,
        in_specs=(
            P(("fsdp", "tp"), None),
            P("fsdp", None),
            P(),
            P(),
            P(None, "fsdp", "tp"),
            P(None, "tp"),
            P("tp", "fsdp"),
            P(),
            P("fsdp", "tp"),
            P("tp"),
            P("tp", "fsdp"),
            P(),
            P(("fsdp", "tp"), None),
        ),
        out_specs=(
            P(("fsdp", "tp"), None),
            P(("fsdp", "tp"), None),
            P(),
            P(),
            P(None, "fsdp", "tp"),
            P(),
            P("tp", "fsdp"),
            P(),
            P("fsdp", "tp"),
            P(),
            P("tp", "fsdp"),
            P(),
        ),
        check_vma=False,
    )
```

```python
import functools
import math

import jax
import jax.numpy as jnp
from jax import lax
from jax.experimental import pallas as pl
from jax.experimental.pallas import tpu as pltpu
from jax.sharding import PartitionSpec as P

D = 2048
HEAD_DIM = 64
ROT = 32
FF = 8192
MIB = 1 << 20

wide = jnp.float32
narrow = jnp.bfloat16
norm_epsilon = 1e-05
masked_score = -1e30


def gelu_tanh(values):
    return (
        0.5
        * values
        * (1.0 + jnp.tanh(0.7978845608028654 * (values + 0.044715 * values * values * values)))
    )


def layer_norm(tokens_in, gain, offset):
    centre = jnp.mean(tokens_in, axis=-1, keepdims=True)
    centred = tokens_in - centre
    spread = jnp.mean(centred * centred, axis=-1, keepdims=True)
    return centred * lax.rsqrt(spread + norm_epsilon) * gain + offset


def lane_constants():
    place = jnp.arange(2 * HEAD_DIM, dtype=jnp.int32) % HEAD_DIM
    turned = (place % (ROT // 2)).astype(wide) * 2.0
    frequency = jnp.exp(turned * (-math.log(10000.0) / ROT))
    sign = jnp.where(place < ROT // 2, -1.0, 1.0)
    inside = place < ROT
    return jnp.stack([jnp.where(inside, frequency, 0.0), jnp.where(inside, sign, 0.0)])


def nt(a, b):
    return lax.dot_general(a, b, (((1,), (1,)), ((), ())), preferred_element_type=wide)


def nn(a, b):
    return lax.dot_general(a, b, (((1,), (0,)), ((), ())), preferred_element_type=wide)


def tn(a, b):
    return lax.dot_general(a, b, (((0,), (0,)), ((), ())), preferred_element_type=wide)


def attention_kernel(
    rows,
    bound_ref,
    cos_ref,
    sin_ref,
    q_ref,
    k_ref,
    v_ref,
    do_ref,
    attn_ref,
    gq_ref,
    gk_ref,
    gv_ref,
    kb_ref,
    vb_ref,
    dk_ref,
    dv_ref,
):
    length = q_ref.shape[0]
    lanes = 2 * HEAD_DIM
    place = lax.broadcasted_iota(jnp.int32, (1, lanes), 1)
    low_half = (place % HEAD_DIM) < (ROT // 2)
    scale = HEAD_DIM**-0.5

    def partner(u):
        return jnp.where(
            low_half, pltpu.roll(u, lanes - ROT // 2, 1), pltpu.roll(u, ROT // 2, 1)
        )

    def turn(u, cosine, sine):
        return u * cosine + partner(u) * sine

    def turn_back(u, cosine, sine):
        return u * cosine - partner(u) * sine

    bound = bound_ref[0, 0:1, 0:1].astype(jnp.int32)
    kb_ref[...] = turn(k_ref[...], cos_ref[...], sin_ref[...]).astype(narrow)
    vb_ref[...] = v_ref[...].astype(narrow)
    dk_ref[...] = jnp.zeros_like(dk_ref)
    dv_ref[...] = jnp.zeros_like(dv_ref)
    for first in range(0, length, rows):
        seen = first + rows
        here = slice(first, seen)
        cosine, sine = cos_ref[here], sin_ref[here]
        q_both = (turn(q_ref[here], cosine, sine).astype(narrow) * scale).astype(narrow)
        row_place = first + lax.broadcasted_iota(jnp.int32, (rows, seen), 0)
        key_place = lax.broadcasted_iota(jnp.int32, (rows, seen), 1)
        row_start = first + lax.broadcasted_iota(jnp.int32, (rows, 1), 0)
        opening = jnp.where(row_start >= bound, bound, 0)
        allowed = (key_place <= row_place) & (key_place >= opening)
        attn_parts, dq_parts, dk_parts, dv_parts = [], [], [], []
        for head in range(2):
            cols = slice(head * HEAD_DIM, (head + 1) * HEAD_DIM)
            q = q_both[:, cols]
            k, v = kb_ref[0:seen, cols], vb_ref[0:seen, cols]
            do = do_ref[here, cols]
            scores = jnp.where(allowed, nt(q, k), masked_score)
            largest = jnp.max(scores, axis=-1, keepdims=True)
            exponent = jnp.exp(scores - largest)
            probs = exponent * (1.0 / jnp.sum(exponent, axis=-1, keepdims=True))
            probs_low = probs.astype(narrow)
            attn_parts.append(nn(probs_low, v))
            grad_probs = nt(do, v)
            inner = jnp.sum(probs * grad_probs, axis=-1, keepdims=True)
            grad_scores = (probs * (grad_probs - inner)).astype(narrow)
            dq_parts.append(nn(grad_scores, k))
            dk_parts.append(tn(grad_scores, q))
            dv_parts.append(tn(probs_low, do))
        attn_ref[here] = jnp.concatenate(attn_parts, axis=1).astype(narrow)
        dq = jnp.concatenate(dq_parts, axis=1) * scale
        gq_ref[here] = turn_back(dq, cosine, sine).astype(narrow)
        dk_ref[0:seen] += jnp.concatenate(dk_parts, axis=1)
        dv_ref[0:seen] += jnp.concatenate(dv_parts, axis=1)
    gk_ref[...] = turn_back(dk_ref[...], cos_ref[...], sin_ref[...]).astype(narrow)
    gv_ref[...] = dv_ref[...].astype(narrow)


def attention(bounds, cosine, sine, projected, grad_attn, length):
    tokens, width = grad_attn.shape
    lanes = 2 * HEAD_DIM
    pairs = width // lanes
    rows = min(256, length)
    bound = pl.BlockSpec((1, 8, 128), lambda s, h: (s, 0, 0))
    table = pl.BlockSpec((length, lanes), lambda s, h: (s, 0))
    block = pl.BlockSpec((length, lanes), lambda s, h: (s, h))
    k_block = pl.BlockSpec((length, lanes), lambda s, h: (s, pairs + h))
    v_block = pl.BlockSpec((length, lanes), lambda s, h: (s, 2 * pairs + h))
    out = jax.ShapeDtypeStruct((tokens, width), narrow)
    return pl.pallas_call(
        functools.partial(attention_kernel, rows),
        grid=(tokens // length, pairs),
        in_specs=[bound, table, table, block, k_block, v_block, block],
        out_specs=[block] * 4,
        out_shape=[out] * 4,
        scratch_shapes=[
            pltpu.VMEM((length, lanes), narrow),
            pltpu.VMEM((length, lanes), narrow),
            pltpu.VMEM((length, lanes), wide),
            pltpu.VMEM((length, lanes), wide),
        ],
        compiler_params=pltpu.CompilerParams(vmem_limit_bytes=48 * MIB),
        cost_estimate=pl.CostEstimate(
            flops=tokens * length * width * 12, bytes_accessed=tokens * width * 32, transcendentals=0
        ),
        name="attention",
    )(bounds, cosine, sine, projected, projected, projected, grad_attn)


MESH = pl.DeviceIdType.MESH


def neighbours():
    f_place, t_place = lax.axis_index("fsdp"), lax.axis_index("tp")
    side, chip, core = f_place % 2, t_place // 2, t_place % 2
    over_x = {"fsdp": f_place + 1 - 2 * side, "tp": t_place}
    over_y = {"fsdp": f_place, "tp": t_place + 2 - 4 * chip}
    over_core = {"fsdp": f_place, "tp": t_place + 1 - 2 * core}
    return side, chip, core, over_x, over_y, over_core


def greet(*others):
    barrier = pltpu.get_barrier_semaphore()
    count = 0
    for other, there in others:
        if there is True:
            pl.semaphore_signal(barrier, inc=1, device_id=other, device_id_type=MESH)
            count = count + 1
        else:

            @pl.when(there)
            def _():
                pl.semaphore_signal(barrier, inc=1, device_id=other, device_id_type=MESH)

            count = count + there.astype(jnp.int32)
    pl.semaphore_wait(barrier, count)


class Copies:
    def __init__(self, send_sems, recv_sems):
        self.send_sems, self.recv_sems, self.count, self.started = send_sems, recv_sems, 0, []

    def remote(self, source, target, device):
        copy = pltpu.make_async_remote_copy(
            src_ref=source,
            dst_ref=target,
            send_sem=self.send_sems.at[self.count],
            recv_sem=self.recv_sems.at[self.count],
            device_id=device,
            device_id_type=MESH,
        )
        self.count += 1
        copy.start()
        self.started.append(copy)
        return copy

    def local(self, source, target):
        copy = pltpu.make_async_copy(source, target, self.send_sems.at[self.count])
        self.count += 1
        copy.start()
        return copy


def half(which, width):
    return pl.ds(pl.multiple_of(which * width, 128), width)


def chain(planes):
    f_place, t_place = lax.axis_index("fsdp"), lax.axis_index("tp")
    plane = f_place // 2
    above = {"fsdp": f_place + 2, "tp": t_place}
    below = {"fsdp": f_place - 2, "tp": t_place}
    return plane, above, below, plane < planes - 1, plane > 0


class PlaneGather:
    def __init__(self, planes, whole, send_sems, recv_sems):
        self.planes, self.whole, self.send_sems, self.recv_sems = planes, whole, send_sems, recv_sems
        self.plane, above, below, has_above, has_below = chain(planes)
        self.side = lax.axis_index("fsdp") % 2
        self.devices, self.has_after = (above, below), (has_above, has_below)

    def spot(self, plane, piece):
        return self.whole.at[plane, self.side if piece == 0 else 1 - self.side]

    def copy(self, way, step, piece, back):
        ref = self.spot(self.plane - back if way == 0 else self.plane + back, piece)
        return pltpu.make_async_remote_copy(
            src_ref=ref,
            dst_ref=ref,
            send_sem=self.send_sems.at[way, step, piece],
            recv_sem=self.recv_sems.at[way, step, piece],
            device_id=self.devices[way],
            device_id_type=MESH,
        )

    def exists(self, way, back):
        return self.plane >= back if way == 0 else self.plane + back < self.planes

    def send(self, step, piece):
        for way in range(2):

            @pl.when(self.has_after[way] & self.exists(way, step - 1))
            def _():
                self.copy(way, step, piece, step - 1).start()

    def receive(self, step, piece):
        for way in range(2):

            @pl.when(self.exists(way, step))
            def _():
                self.copy(way, step, piece, step).wait_recv()

    def drain(self):
        for step in range(1, self.planes):
            for piece in range(2):
                for way in range(2):

                    @pl.when(self.has_after[way] & self.exists(way, step - 1))
                    def _():
                        self.copy(way, step, piece, step - 1).wait_send()


def gather_kernel(
    planes,
    input_ref,
    segment_ref,
    gain_ref,
    bias_ref,
    w_out_ref,
    w_fc2_ref,
    lane_ref,
    given_ref,
    qkv_ref,
    fc1_ref,
    normed_all,
    given_all,
    qo_all,
    fc1_block,
    fc2_ref,
    bound_ref,
    cos_ref,
    sin_ref,
    normed_ref,
    out_ref,
    send_sems,
    recv_sems,
    plane_send_sems,
    plane_recv_sems,
):
    side, chip, core, over_x, over_y, over_core = neighbours()
    plane, above, below, has_above, has_below = chain(planes)
    rows = input_ref.shape[0]
    cut = rows // 2
    length = segment_ref.shape[1]
    out_ref[...] = w_out_ref[...].T
    zeros = length - jnp.sum(segment_ref[...], axis=1, keepdims=True)
    bound_ref[side] = jnp.broadcast_to(zeros.astype(wide), bound_ref.shape[1:])
    greet(
        (over_x, True), (over_y, True), (over_core, True), (above, has_above), (below, has_below)
    )
    copies = Copies(send_sems, recv_sems)

    width = out_ref.shape[1] // 2
    qo = PlaneGather(planes, qo_all, plane_send_sems, plane_recv_sems)
    qo_kept, qo_came = [], []
    for part in range(4):
        source = qkv_ref.at[part] if part < 3 else out_ref
        target = qo_all.at[plane, side, :, pl.ds(part * width, width)]
        qo_kept.append(copies.local(source.at[:, half(side, width)], target))
        qo_came.append(copies.remote(source.at[:, half(1 - side, width)], target, over_x))
    bounds = copies.remote(bound_ref.at[side], bound_ref.at[side], over_x)
    mine = [whole.at[side, chip, core] for whole in (normed_all, given_all)]
    y_given = copies.remote(given_ref, mine[1], over_y)
    for copy in qo_kept:
        copy.wait()
    qo.send(1, 0)

    tokens = input_ref[...].astype(wide)
    normed_ref[...] = layer_norm(tokens, gain_ref[...], bias_ref[...]).astype(narrow)
    x_normed = copies.remote(normed_ref, mine[0], over_x)
    y_normed = copies.remote(normed_ref, mine[0], over_y)
    kept = [copies.local(normed_ref, mine[0]), copies.local(given_ref, mine[1])]
    last = [
        copies.remote(normed_ref, mine[0], over_core),
        copies.remote(given_ref, mine[1], over_core),
    ]
    for copy in qo_came:
        copy.wait_recv()
    qo.send(1, 1)
    x_given = copies.remote(given_ref, mine[1], over_x)
    ff_width = fc1_ref.shape[1] // 2
    kept.append(copies.local(fc1_ref.at[:, half(side, ff_width)], fc1_block.at[side]))

    bounds.wait_recv()
    step = min(256, length)

    def tables(i, carry):
        here = pl.ds(pl.multiple_of(i * step, 8), step)
        sequence, first = i // (length // step), (i % (length // step)) * step
        place = (first + lax.broadcasted_iota(jnp.int32, (step, 1), 0)).astype(wide)
        bound = bound_ref[sequence, 0:1, 0:1]
        angles = (place - jnp.where(place >= bound, bound, 0.0)) * lane_ref[0:1]
        cos_ref[here] = jnp.cos(angles)
        sin_ref[here] = jnp.sin(angles) * lane_ref[1:2]
        return carry

    lax.fori_loop(0, 2 * length // step, tables, 0)

    def forward(step):
        for piece in range(2):
            qo.receive(step - 1, piece)
            qo.send(step, piece)

    if planes > 2:
        forward(2)
    fc2_ref[...] = w_fc2_ref[...].T
    y_slot = [whole.at[side, 1 - chip, core] for whole in (normed_all, given_all)]
    x_slot = [whole.at[1 - side, chip, core] for whole in (normed_all, given_all)]
    x_normed.wait_recv()
    corner = [[copies.remote(x_slot[0], x_slot[0], over_y)]]
    last.append(copies.remote(x_slot[0], x_slot[0], over_core))
    y_given.wait_recv()
    part = y_slot[1].at[pl.ds(0, cut)]
    corner.append([copies.remote(part, part, over_x)])
    last.append(
        copies.remote(fc1_ref.at[:, half(1 - side, ff_width)], fc1_block.at[side], over_x)
    )
    last.append(copies.remote(y_slot[1], y_slot[1], over_core))
    for k in range(3, planes):
        forward(k)
    y_normed.wait_recv()
    last.append(copies.remote(y_slot[0], y_slot[0], over_core))
    x_given.wait_recv()
    part = x_slot[1].at[pl.ds(cut, rows - cut)]
    corner[1].append(copies.remote(part, part, over_y))
    last.append(copies.remote(x_slot[1], x_slot[1], over_core))
    for whole, parts in zip((normed_all, given_all), corner):
        for copy in parts:
            copy.wait_recv()
        slot = whole.at[1 - side, 1 - chip, core]
        last.append(copies.remote(slot, slot, over_core))
    for piece in range(2):
        qo.receive(planes - 1, piece)
    for copy in kept:
        copy.wait()
    for copy in copies.started:
        copy.wait_send()
    qo.drain()
    for copy in last:
        copy.wait_recv()


def gather_tokens(planes, inputs, segments, gain, bias, given, w_qkv, w_out, fc1, w_fc2):
    mine, rows, lanes = inputs.shape[0], fc1.shape[0], 2 * HEAD_DIM
    tokens, length = 8 * mine, segments.shape[1]
    columns = 2 * w_out.shape[0]
    whole = jax.ShapeDtypeStruct((2, 2, 2, mine, D), narrow)
    block = jax.ShapeDtypeStruct((2, rows, fc1.shape[1] // 2), narrow)
    table = jax.ShapeDtypeStruct((2 * length, lanes), wide)
    weights = jax.ShapeDtypeStruct((planes, 2, rows, columns), narrow)
    anywhere, vmem = pl.BlockSpec(memory_space=pl.ANY), pl.BlockSpec(memory_space=pltpu.VMEM)
    normed_all, given_all, qo_all, fc1_block, fc2_rows, bounds, cosine, sine = pl.pallas_call(
        functools.partial(gather_kernel, planes),
        in_specs=[vmem] * 7 + [anywhere] * 3,
        out_specs=[anywhere] * 4 + [vmem] * 4,
        out_shape=[
            whole,
            whole,
            weights,
            block,
            jax.ShapeDtypeStruct((rows, w_fc2.shape[0]), narrow),
            jax.ShapeDtypeStruct((2, 8, 128), wide),
            table,
            table,
        ],
        scratch_shapes=[
            pltpu.VMEM((mine, D), narrow),
            pltpu.VMEM((rows, w_out.shape[0]), narrow),
            pltpu.SemaphoreType.DMA((32,)),
            pltpu.SemaphoreType.DMA((32,)),
            pltpu.SemaphoreType.DMA((2, planes, 2)),
            pltpu.SemaphoreType.DMA((2, planes, 2)),
        ],
        compiler_params=pltpu.CompilerParams(
            collective_id=1, has_side_effects=True, vmem_limit_bytes=32 * MIB
        ),
        name="gather_tokens",
    )(inputs, segments, gain, bias, w_out, w_fc2, lane_constants(), given, w_qkv, fc1)
    return (
        normed_all.reshape(tokens, D),
        given_all.reshape(tokens, D),
        qo_all.reshape(D, columns),
        fc1_block,
        fc2_rows,
        bounds,
        cosine,
        sine,
    )


def scatter_kernel(planes, which, *refs):
    lefts = sorted(set(which))
    n_left, n_right = len(lefts), len(which)
    left_refs, right_refs = refs[:n_left], refs[n_left : n_left + n_right]
    (
        fc1_ref,
        bias_ref,
        weight_ref,
        out_ref,
        weight_all,
        active_all,
        slope_all,
        grad_all,
        left_vmem,
        turned,
        going,
        came,
        active_stage,
        slope_stage,
        grad_stage,
        load_sems,
        send_sems,
        recv_sems,
        x_send_sems,
        x_recv_sems,
        store_sems,
    ) = refs[n_left + n_right :]
    side, _, _, over_x, _, _ = neighbours()
    plane, above, below, has_above, has_below = chain(planes)
    devices, has_after, has_before = (above, below), (has_above, has_below), (has_below, has_above)
    group, width = out_ref.shape[1], right_refs[0].shape[1]
    tokens = right_refs[0].shape[0]
    own = out_ref

    def load(j):
        return [
            pltpu.make_async_copy(
                left_refs[i].at[:, pl.ds(pl.multiple_of(j * group, 128), group)],
                left_vmem.at[i, j],
                load_sems.at[i, j],
            )
            for i in range(n_left)
        ]

    def order(k):
        return jnp.where(plane < planes // 2, planes - 1 - k, k)

    for k in range(planes):
        for copy in load(order(k)):
            copy.start()
    greet((over_x, True), (above, has_above), (below, has_below))
    copies = Copies(x_send_sems, x_recv_sems)
    columns = weight_ref.shape[1] // 2
    kept = copies.local(weight_ref.at[:, half(side, columns)], weight_all.at[plane, side])
    other = copies.remote(
        weight_ref.at[:, half(1 - side, columns)], weight_all.at[plane, side], over_x
    )

    def depth(way):
        return plane if way == 0 else planes - 1 - plane

    def named(way, block):
        return block if way == 0 else planes - 1 - block

    def is_weight(at, number):
        return (number <= at) | (number == at + 2)

    def weight_block(at, number):
        return jnp.where(number <= at, at - number + 1, 0)

    def sum_block(at, number):
        return jnp.where(number == at + 1, planes - 1, planes + 1 + at - number)

    def weight_copies(way, number, at, pieces=(0, 1)):
        j = named(way, weight_block(at, number))
        return [
            pltpu.make_async_remote_copy(
                src_ref=weight_all.at[j, piece_side],
                dst_ref=weight_all.at[j, piece_side],
                send_sem=send_sems.at[way, number, piece],
                recv_sem=recv_sems.at[way, number, piece],
                device_id=devices[way],
                device_id_type=MESH,
            )
            for piece, piece_side in enumerate((side, 1 - side))
            if piece in pieces
        ]

    def landing(way, j, receiver):
        return j if way == 0 else jnp.where(j == receiver, planes, j)

    def sum_copy(way, number, at, receiver, arriving):
        j = named(way, sum_block(at, number))
        spot = landing(way, j, receiver)
        return j, spot, pltpu.make_async_remote_copy(
            src_ref=came.at[spot] if arriving else going.at[j],
            dst_ref=came.at[spot],
            send_sem=send_sems.at[way, number, 2],
            recv_sem=recv_sems.at[way, number, 2],
            device_id=devices[way],
            device_id_type=MESH,
        )

    def next_plane(way):
        return plane + 1 if way == 0 else plane - 1

    def finish_send(way, number):
        at = depth(way)

        @pl.when(has_after[way] & is_weight(at, number))
        def _():
            for copy in weight_copies(way, number, at):
                copy.wait_send()

        @pl.when(has_after[way] & jnp.logical_not(is_weight(at, number)))
        def _():
            sum_copy(way, number, at, next_plane(way), False)[2].wait_send()

    def take(way, number):
        at = depth(way) - 1

        @pl.when(has_before[way] & is_weight(at, number))
        def _():
            for copy in weight_copies(way, number, at):
                copy.wait_recv()

        @pl.when(has_before[way] & jnp.logical_not(is_weight(at, number)))
        def _():
            j, spot, copy = sum_copy(way, number, at, plane, True)
            copy.wait_recv()

            @pl.when(j == plane)
            def _():
                own[...] += came[spot].astype(wide)

            @pl.when(j != plane)
            def _():
                going[j] = (going[j].astype(wide) + came[spot].astype(wide)).astype(narrow)

    def give(way, number):
        at = depth(way)

        @pl.when(has_after[way] & is_weight(at, number))
        def _():
            for copy in weight_copies(way, number, at):
                copy.start()

        @pl.when(has_after[way] & jnp.logical_not(is_weight(at, number)))
        def _():
            sum_copy(way, number, at, next_plane(way), False)[2].start()

    step = slope_stage.shape[1]
    blocks = tokens // step

    def turn(i, carry):
        here = pl.ds(pl.multiple_of(i * step, 128), step)
        for number, right_ref in enumerate(right_refs):
            turned[number * width : (number + 1) * width, here] = right_ref[here].T
        return carry

    def multiply(k):
        j = order(k)
        for copy in load(j):
            copy.wait()
        for i in range(n_left):
            numbers = [number for number, left in enumerate(which) if left == lefts[i]]
            here = slice(numbers[0] * width, (numbers[-1] + 1) * width)
            block = nn(turned[here], left_vmem[i, j])
            going[j, here] = block.astype(narrow)

            @pl.when(j == plane)
            def _():
                own[here] = block

    def store_hidden(i, slot):
        here = pl.ds(pl.multiple_of(i * step, 16), step)
        return [
            pltpu.make_async_copy(slope_stage.at[slot], slope_all.at[here], store_sems.at[0, slot]),
            pltpu.make_async_copy(active_stage.at[slot], active_all.at[here], store_sems.at[1, slot]),
        ]

    def hidden_units(i, carry):
        here = pl.ds(pl.multiple_of(i * step, 128), step)
        slot = i % 2
        hidden = bias_ref[...] + nn(left_vmem[0, 0, here], fc1_ref[0:group])
        for j in range(1, planes):
            hidden += nn(left_vmem[0, j, here], fc1_ref[j * group : (j + 1) * group])
        squared = hidden * hidden
        inner = jnp.tanh(0.7978845608028654 * hidden * (1.0 + 0.044715 * squared))
        half_sum = 0.5 * (1.0 + inner)
        active = (hidden * half_sum).astype(narrow)

        @pl.when(i >= 2)
        def _():
            for copy in store_hidden(i - 2, slot):
                copy.wait()

        active_stage[slot] = active
        slope_stage[slot] = half_sum + hidden * (0.5 * (1.0 - inner * inner)) * (
            0.7978845608028654 * (1.0 + 3.0 * 0.044715 * squared)
        )
        for copy in store_hidden(i, slot):
            copy.start()
        turned[:, here] = active.T
        return carry

    def store_grad(j, slot):
        return pltpu.make_async_copy(grad_stage.at[slot], grad_all.at[j], store_sems.at[2, slot])

    def fc2_gradient(j, carry):
        slot = j % 2

        @pl.when(j >= 2)
        def _():
            store_grad(j - 2, slot).wait()

        grad_stage[slot] = nn(turned[...], left_vmem[n_left - 1, j]).astype(narrow)
        store_grad(j, slot).start()
        return carry

    kept.wait()
    for way in range(2):

        @pl.when(has_after[way] & (depth(way) > 0))
        def _():
            weight_copies(way, 1, depth(way), (0,))[0].start()

    lax.fori_loop(0, blocks, turn, 0)
    multiply(0)
    for way in range(2):

        @pl.when(has_after[way] & (depth(way) == 0))
        def _():
            sum_copy(way, 1, 0, next_plane(way), False)[2].start()

    other.wait_recv()
    for way in range(2):

        @pl.when(has_after[way] & (depth(way) > 0))
        def _():
            weight_copies(way, 1, depth(way), (1,))[0].start()

    for k in range(1, planes):
        multiply(k)

    lax.fori_loop(0, blocks // 2, hidden_units, 0)
    for number in range(2, planes + 1):
        for way in range(2):
            take(way, number - 1)
            finish_send(way, number - 1)
            give(way, number)
        if number == 2:
            lax.fori_loop(blocks // 2, blocks, hidden_units, 0)
            lax.fori_loop(0, planes // 2, fc2_gradient, 0)
        if number == min(3, planes):
            lax.fori_loop(planes // 2, planes, fc2_gradient, 0)
    for way in range(2):
        take(way, planes)
    for way in range(2):
        finish_send(way, planes)
    for slot in range(2):
        for copy in store_hidden(blocks - 2 + slot, slot) + [store_grad(planes - 2 + slot, slot)]:
            copy.wait()
    for copy in copies.started:
        copy.wait_send()


def backward_step(planes, lefts, rights, which, fc1, bias, weight, collective_id):
    tokens, width = rights[0].shape
    group, columns, hidden = D // planes, width * len(rights), fc1.shape[1]
    rows, step = group // 2, min(256, tokens // 2)
    anywhere, vmem = pl.BlockSpec(memory_space=pl.ANY), pl.BlockSpec(memory_space=pltpu.VMEM)
    total, weight_all, active, slope, grad = pl.pallas_call(
        functools.partial(scatter_kernel, planes, which),
        in_specs=[anywhere] * len(lefts) + [vmem] * (len(rights) + 2) + [anywhere],
        out_specs=[vmem] + [anywhere] * 4,
        out_shape=[
            jax.ShapeDtypeStruct((columns, group), wide),
            jax.ShapeDtypeStruct((planes, 2, rows, weight.shape[1] // 2), narrow),
            jax.ShapeDtypeStruct((tokens, hidden), narrow),
            jax.ShapeDtypeStruct((tokens, hidden), wide),
            jax.ShapeDtypeStruct((planes, hidden, group), narrow),
        ],
        scratch_shapes=[
            pltpu.VMEM((len(lefts), planes, tokens, group), narrow),
            pltpu.VMEM((columns, tokens), narrow),
            pltpu.VMEM((planes, columns, group), narrow),
            pltpu.VMEM((planes + 1, columns, group), narrow),
            pltpu.VMEM((2, step, hidden), narrow),
            pltpu.VMEM((2, step, hidden), wide),
            pltpu.VMEM((2, hidden, group), narrow),
            pltpu.SemaphoreType.DMA((len(lefts), planes)),
            pltpu.SemaphoreType.DMA((2, planes + 1, 3)),
            pltpu.SemaphoreType.DMA((2, planes + 1, 3)),
            pltpu.SemaphoreType.DMA((2,)),
            pltpu.SemaphoreType.DMA((2,)),
            pltpu.SemaphoreType.DMA((3, 2)),
        ],
        compiler_params=pltpu.CompilerParams(
            collective_id=collective_id, has_side_effects=True, vmem_limit_bytes=62 * MIB
        ),
        cost_estimate=pl.CostEstimate(
            flops=40 * tokens * D * columns, bytes_accessed=2 * tokens * D, transcendentals=0
        ),
        name="backward_step",
    )(*lefts, *rights, fc1, bias, weight)
    return total, weight_all.reshape(D, weight.shape[1] // 2), active, slope, grad


def project_kernel(normed_ref, given_ref, in_ref, out_ref, bias_ref, projected_ref, given_attn_ref):
    projected_ref[...] = nn(normed_ref[...], in_ref[...]) + bias_ref[...]
    given_attn_ref[...] = nn(given_ref[...], out_ref[...]).astype(narrow)


def project(normed, given, weights, bias):
    tokens, width = normed.shape[0], weights.shape[1] // 4
    block = min(256, tokens)
    row = pl.BlockSpec((block, D), lambda i: (i, 0))
    return pl.pallas_call(
        project_kernel,
        grid=(tokens // block,),
        in_specs=[
            row,
            row,
            pl.BlockSpec((D, 3 * width), lambda i: (0, 0)),
            pl.BlockSpec((D, width), lambda i: (0, 3)),
            pl.BlockSpec((1, 3 * width), lambda i: (0, 0)),
        ],
        out_specs=[
            pl.BlockSpec((block, 3 * width), lambda i: (i, 0)),
            pl.BlockSpec((block, width), lambda i: (i, 0)),
        ],
        out_shape=[
            jax.ShapeDtypeStruct((tokens, 3 * width), wide),
            jax.ShapeDtypeStruct((tokens, width), narrow),
        ],
        compiler_params=pltpu.CompilerParams(vmem_limit_bytes=48 * MIB),
        cost_estimate=pl.CostEstimate(
            flops=8 * tokens * D * width, bytes_accessed=8 * tokens * D, transcendentals=0
        ),
        name="project",
    )(normed, given, weights, weights, bias)


def product_kernel(count, *refs):
    total = nt(refs[0][...], refs[count][...])
    for number in range(1, count):
        total += nt(refs[number][...], refs[count + number][...])
    refs[2 * count][...] = total.astype(narrow)


def sum_of_products(pairs):
    tokens = pairs[0][0].shape[0]
    block = min(256, tokens)
    left = [pl.BlockSpec((block, a.shape[1]), lambda i: (i, 0)) for a, _, _ in pairs]
    right = [
        pl.BlockSpec((w.shape[0], a.shape[1]), functools.partial(lambda c, i: (0, c), c))
        for a, w, c in pairs
    ]
    depth = sum(a.shape[1] for a, _, _ in pairs)
    return pl.pallas_call(
        functools.partial(product_kernel, len(pairs)),
        grid=(tokens // block,),
        in_specs=left + right,
        out_specs=pl.BlockSpec((block, D), lambda i: (i, 0)),
        out_shape=jax.ShapeDtypeStruct((tokens, D), narrow),
        compiler_params=pltpu.CompilerParams(vmem_limit_bytes=48 * MIB),
        cost_estimate=pl.CostEstimate(
            flops=2 * tokens * depth * D, bytes_accessed=2 * depth * (tokens + D), transcendentals=0
        ),
        name="sum_of_products",
    )(*[a for a, _, _ in pairs], *[w for _, w, _ in pairs])


def solution(mesh):
    nf = mesh.shape["fsdp"]
    nt_axis = mesh.shape["tp"]
    columns_of_planes = [list(range(side, nf, 2)) for side in range(2)]
    swap_f = [(f, f ^ 1) for f in range(nf)]
    swap_core = [(t, t ^ 1) for t in range(nt_axis)]
    swap_chip = [(t, t ^ 2) for t in range(nt_axis)]

    def send_x(v):
        return lax.ppermute(v, "fsdp", swap_f)

    def send_y(v):
        return lax.ppermute(v, "tp", swap_chip)

    def send_core(v):
        return lax.ppermute(v, "tp", swap_core)

    def gather_planes(block):
        block = block.reshape(block.shape[0] * block.shape[1], block.shape[2])
        return lax.all_gather(
            block, "fsdp", axis=0, tiled=True, axis_index_groups=columns_of_planes
        )

    def local(
        inputs,
        segments,
        ln_gain,
        ln_bias,
        w_qkv,
        b_qkv,
        w_out,
        b_out,
        w_fc1,
        b_fc1,
        w_fc2,
        b_fc2,
        cotangent,
    ):
        f_place = lax.axis_index("fsdp")
        t_place = lax.axis_index("tp")
        side = f_place % 2
        chip, core = t_place // 2, t_place % 2
        length = segments.shape[1]
        mine = inputs.shape[0]
        rows = w_fc1.shape[0]
        half_qkv, half_ff = w_qkv.shape[2] // 2, w_fc1.shape[1] // 2

        def pick(v, index, axis=0):
            return lax.dynamic_index_in_dim(v, index, axis, keepdims=False)

        def in_order(kept, came):
            return jnp.where(side == 0, jnp.stack([kept, came]), jnp.stack([came, kept]))

        def sum_planes(grads):
            return lax.psum_scatter(
                grads.astype(narrow),
                "fsdp",
                scatter_dimension=0,
                tiled=True,
                axis_index_groups=columns_of_planes,
            )

        def halves_of(kept, came):
            return in_order(kept, came).astype(wide)

        def scatter_sides(total):
            parts = total.astype(narrow).reshape(total.shape[0], 2, rows)
            return halves_of(pick(parts, side, 1), send_x(pick(parts, 1 - side, 1)))

        def scatter_tokens(total):
            parts = total.reshape(2, 2, 2, mine, D)
            came = send_core(pick(parts, 1 - core, 2).astype(narrow))
            summed = pick(parts, core, 2).astype(wide) + came.astype(wide)
            halves = []
            for number, columns in enumerate((summed[..., : D // 2], summed[..., D // 2 :])):
                if number == 0:
                    came = send_x(pick(columns, 1 - side, 0).astype(narrow))
                    part = pick(columns, side, 0) + came.astype(wide)
                    came = send_y(pick(part, 1 - chip, 0).astype(narrow))
                    part = pick(part, chip, 0) + came.astype(wide)
                else:
                    came = send_y(pick(columns, 1 - chip, 1).astype(narrow))
                    part = pick(columns, chip, 1) + came.astype(wide)
                    came = send_x(pick(part, 1 - side, 0).astype(narrow))
                    part = pick(part, side, 0) + came.astype(wide)
                halves.append(part)
            return jnp.concatenate(halves, axis=1)

        def reduce_all(v):
            for axis, size in (("tp", nt_axis), ("fsdp", nf)):
                bit = 1
                while bit < size:
                    v = v + lax.ppermute(v, axis, [(i, i ^ bit) for i in range(size)])
                    bit *= 2
            return v

        normed, grad_rows, full_qo, fc1_block, fc2_rows, bounds, cosine, sine = gather_tokens(
            nf // 2,
            inputs,
            segments,
            ln_gain.astype(wide).reshape(1, D),
            ln_bias.astype(wide).reshape(1, D),
            cotangent,
            w_qkv,
            w_out,
            w_fc1,
            w_fc2,
        )
        full_fc1 = gather_planes(fc1_block)
        tokens_in = inputs.astype(wide)
        _, norm_back = jax.vjp(
            layer_norm, tokens_in, ln_gain.astype(wide), ln_bias.astype(wide)
        )

        bias_qkv = lax.dynamic_slice_in_dim(b_qkv, side * half_qkv, half_qkv, axis=1)
        bias_fc1 = lax.dynamic_slice_in_dim(b_fc1, side * half_ff, half_ff, axis=0)

        projected, grad_mixed = project(
            normed, grad_rows, full_qo, bias_qkv.astype(wide).reshape(1, 3 * half_qkv)
        )
        mixed, grad_q, grad_k, grad_v = attention(
            bounds, cosine, sine, projected, grad_mixed, length
        )
        sum_qo, full_fc2, active_low, slope, grad_w2 = backward_step(
            nf // 2,
            [normed, grad_rows],
            [grad_q, grad_k, grad_v, mixed],
            (0, 0, 0, 1),
            full_fc1,
            bias_fc1.astype(wide).reshape(1, half_ff),
            fc2_rows,
            2,
        )
        sum_fc2 = scatter_sides(sum_planes(grad_w2.reshape(-1, grad_w2.shape[2])))
        grad_hidden = (nn(grad_rows, full_fc2) * slope).astype(narrow)
        grad_w1 = tn(normed, grad_hidden).astype(narrow)
        total_fc1 = sum_planes(grad_w1)
        grad_hidden, mixed, grad_w1 = lax.optimization_barrier((grad_hidden, mixed, grad_w1))
        grad_projected = jnp.concatenate([grad_q, grad_k, grad_v], axis=1)
        grad_normed = scatter_tokens(
            sum_of_products(
                [(grad_q, full_qo, 0), (grad_k, full_qo, 1), (grad_v, full_qo, 2), (grad_hidden, full_fc1, 0)]
            )
        )
        branch_local = scatter_tokens(
            sum_of_products([(mixed, full_qo, 3), (active_low, full_fc2, 0)])
        )
        outputs = (tokens_in + branch_local + b_out.astype(wide) + b_fc2.astype(wide)).astype(narrow)
        grad_tokens, grad_gain, grad_offset = norm_back(grad_normed)
        grad_tokens = grad_tokens + cotangent.astype(wide)

        sum_qo = scatter_sides(sum_qo)
        grad_w_qkv = sum_qo[:, : 3 * half_qkv].reshape(2, 3, half_qkv, rows)
        grad_w_qkv = grad_w_qkv.transpose(1, 3, 0, 2).reshape(3, rows, 2 * half_qkv)
        grad_w_out = sum_qo[:, 3 * half_qkv :].reshape(2 * half_qkv, rows)
        grad_w_fc2 = sum_fc2.reshape(2 * half_ff, rows)

        anchor = jnp.zeros((), jnp.int32)
        bias_qkv_full = lax.dynamic_update_slice(
            jnp.zeros((3, D), wide),
            jnp.sum(grad_projected.astype(wide), axis=0).reshape(3, half_qkv),
            (anchor, (2 * t_place + side) * half_qkv),
        )
        bias_fc1_full = lax.dynamic_update_slice(
            jnp.zeros((FF,), wide),
            jnp.sum(grad_hidden.astype(wide), axis=0),
            ((2 * t_place + side) * half_ff,),
        )
        cotangent_sum = jnp.sum(cotangent.astype(wide), axis=0)
        small = reduce_all(
            jnp.concatenate(
                [bias_qkv_full.reshape(-1), bias_fc1_full, grad_gain, grad_offset, cotangent_sum]
            ).reshape(-1, 128)
        ).reshape(-1)
        total_fc1, outputs, grad_tokens, small, grad_w_qkv, grad_w_out, grad_w_fc2 = (
            lax.optimization_barrier(
                (total_fc1, outputs, grad_tokens, small, grad_w_qkv, grad_w_out, grad_w_fc2)
            )
        )
        parts = total_fc1.reshape(2, rows, total_fc1.shape[1])
        kept, came = pick(parts, side).astype(wide), send_x(pick(parts, 1 - side)).astype(wide)
        grad_w_fc1 = jnp.where(
            side == 0,
            jnp.concatenate([kept, came], axis=1),
            jnp.concatenate([came, kept], axis=1),
        )
        total_qkv = small[: 3 * D].reshape(3, D)
        total_b_fc1 = small[3 * D : 3 * D + FF]
        total_gain, total_offset, total_out = small[3 * D + FF :].reshape(3, D)
        return (
            outputs,
            grad_tokens,
            total_gain,
            total_offset,
            grad_w_qkv,
            total_qkv,
            grad_w_out,
            total_out,
            grad_w_fc1,
            total_b_fc1,
            grad_w_fc2,
            total_out,
        )

    return jax.shard_map(
        local,
        mesh=mesh,
        in_specs=(
            P(("fsdp", "tp"), None),
            P("fsdp", None),
            P(),
            P(),
            P(None, "fsdp", "tp"),
            P(None, "tp"),
            P("tp", "fsdp"),
            P(),
            P("fsdp", "tp"),
            P("tp"),
            P("tp", "fsdp"),
            P(),
            P(("fsdp", "tp"), None),
        ),
        out_specs=(
            P(("fsdp", "tp"), None),
            P(("fsdp", "tp"), None),
            P(),
            P(),
            P(None, "fsdp", "tp"),
            P(),
            P("tp", "fsdp"),
            P(),
            P("fsdp", "tp"),
            P(),
            P("tp", "fsdp"),
            P(),
        ),
        check_vma=False,
    )
```

```python
import functools
import math

import jax
import jax.numpy as jnp
from jax import lax
from jax.experimental import pallas as pl
from jax.experimental.pallas import tpu as pltpu
from jax.sharding import PartitionSpec as P

D = 2048
HEAD_DIM = 64
ROT = 32
FF = 8192
VMEM = 62 << 20

wide = jnp.float32
narrow = jnp.bfloat16
norm_epsilon = 1e-05
masked_score = -1e30


def gelu_tanh(values):
    return (
        0.5
        * values
        * (1.0 + jnp.tanh(0.7978845608028654 * (values + 0.044715 * values * values * values)))
    )


def layer_norm(tokens_in, gain, offset):
    centre = jnp.mean(tokens_in, axis=-1, keepdims=True)
    centred = tokens_in - centre
    spread = jnp.mean(centred * centred, axis=-1, keepdims=True)
    return centred * lax.rsqrt(spread + norm_epsilon) * gain + offset


def lane_constants():
    place = lax.broadcasted_iota(jnp.int32, (1, 2 * HEAD_DIM), 1) % HEAD_DIM
    turned = (place % (ROT // 2)).astype(wide) * 2.0
    frequency = jnp.exp(turned * (-math.log(10000.0) / ROT))
    sign = jnp.where(place < ROT // 2, -1.0, 1.0)
    inside = place < ROT
    return jnp.where(inside, frequency, 0.0), jnp.where(inside, sign, 0.0)


def nt(a, b):
    return lax.dot_general(a, b, (((1,), (1,)), ((), ())), preferred_element_type=wide)


def nn(a, b):
    return lax.dot_general(a, b, (((1,), (0,)), ((), ())), preferred_element_type=wide)


def tn(a, b):
    return lax.dot_general(a, b, (((0,), (0,)), ((), ())), preferred_element_type=wide)


def attention_kernel(
    rows,
    bound_ref,
    cos_ref,
    sin_ref,
    q_ref,
    k_ref,
    v_ref,
    do_ref,
    attn_ref,
    gq_ref,
    gk_ref,
    gv_ref,
    kb_ref,
    vb_ref,
    dk_ref,
    dv_ref,
):
    length = q_ref.shape[0]
    lanes = 2 * HEAD_DIM
    place = lax.broadcasted_iota(jnp.int32, (1, lanes), 1)
    low_half = (place % HEAD_DIM) < (ROT // 2)
    scale = HEAD_DIM**-0.5

    def partner(u):
        return jnp.where(
            low_half, pltpu.roll(u, lanes - ROT // 2, 1), pltpu.roll(u, ROT // 2, 1)
        )

    def turn(u, cosine, sine):
        return u * cosine + partner(u) * sine

    def turn_back(u, cosine, sine):
        return u * cosine - partner(u) * sine

    bound = bound_ref[0, 0:1, 0:1].astype(jnp.int32)
    kb_ref[...] = turn(k_ref[...], cos_ref[...], sin_ref[...]).astype(narrow)
    vb_ref[...] = v_ref[...].astype(narrow)
    dk_ref[...] = jnp.zeros_like(dk_ref)
    dv_ref[...] = jnp.zeros_like(dv_ref)
    for first in range(0, length, rows):
        seen = first + rows
        here = slice(first, seen)
        cosine, sine = cos_ref[here], sin_ref[here]
        q_both = (turn(q_ref[here], cosine, sine).astype(narrow) * scale).astype(narrow)
        row_place = first + lax.broadcasted_iota(jnp.int32, (rows, seen), 0)
        key_place = lax.broadcasted_iota(jnp.int32, (rows, seen), 1)
        row_start = first + lax.broadcasted_iota(jnp.int32, (rows, 1), 0)
        opening = jnp.where(row_start >= bound, bound, 0)
        allowed = (key_place <= row_place) & (key_place >= opening)
        attn_parts, dq_parts, dk_parts, dv_parts = [], [], [], []
        for head in range(2):
            cols = slice(head * HEAD_DIM, (head + 1) * HEAD_DIM)
            q = q_both[:, cols]
            k, v = kb_ref[0:seen, cols], vb_ref[0:seen, cols]
            do = do_ref[here, cols]
            scores = jnp.where(allowed, nt(q, k), masked_score)
            largest = jnp.max(scores, axis=-1, keepdims=True)
            exponent = jnp.exp(scores - largest)
            probs = exponent * (1.0 / jnp.sum(exponent, axis=-1, keepdims=True))
            probs_low = probs.astype(narrow)
            attn_parts.append(nn(probs_low, v))
            grad_probs = nt(do, v)
            inner = jnp.sum(probs * grad_probs, axis=-1, keepdims=True)
            grad_scores = (probs * (grad_probs - inner)).astype(narrow)
            dq_parts.append(nn(grad_scores, k))
            dk_parts.append(tn(grad_scores, q))
            dv_parts.append(tn(probs_low, do))
        attn_ref[here] = jnp.concatenate(attn_parts, axis=1).astype(narrow)
        dq = jnp.concatenate(dq_parts, axis=1) * scale
        gq_ref[here] = turn_back(dq, cosine, sine).astype(narrow)
        dk_ref[0:seen] += jnp.concatenate(dk_parts, axis=1)
        dv_ref[0:seen] += jnp.concatenate(dv_parts, axis=1)
    gk_ref[...] = turn_back(dk_ref[...], cos_ref[...], sin_ref[...]).astype(narrow)
    gv_ref[...] = dv_ref[...].astype(narrow)


def attention(bounds, cosine, sine, projected, grad_attn, length):
    tokens, width = grad_attn.shape
    lanes = 2 * HEAD_DIM
    pairs = width // lanes
    rows = min(256, length)
    bound = pl.BlockSpec((1, 8, 128), lambda s, h: (s, 0, 0))
    table = pl.BlockSpec((length, lanes), lambda s, h: (s, 0))
    block = pl.BlockSpec((length, lanes), lambda s, h: (s, h))
    k_block = pl.BlockSpec((length, lanes), lambda s, h: (s, pairs + h))
    v_block = pl.BlockSpec((length, lanes), lambda s, h: (s, 2 * pairs + h))
    out = jax.ShapeDtypeStruct((tokens, width), narrow)
    return pl.pallas_call(
        functools.partial(attention_kernel, rows),
        grid=(tokens // length, pairs),
        in_specs=[bound, table, table, block, k_block, v_block, block],
        out_specs=[block] * 4,
        out_shape=[out] * 4,
        scratch_shapes=[
            pltpu.VMEM((length, lanes), narrow),
            pltpu.VMEM((length, lanes), narrow),
            pltpu.VMEM((length, lanes), wide),
            pltpu.VMEM((length, lanes), wide),
        ],
        compiler_params=pltpu.CompilerParams(vmem_limit_bytes=VMEM),
        cost_estimate=pl.CostEstimate(
            flops=tokens * length * width * 12, bytes_accessed=tokens * width * 32, transcendentals=0
        ),
        name="attention",
    )(bounds, cosine, sine, projected, projected, projected, grad_attn)


MESH = pl.DeviceIdType.MESH


def neighbours():
    f_place, t_place = lax.axis_index("fsdp"), lax.axis_index("tp")
    side, chip, core = f_place % 2, t_place // 2, t_place % 2
    over_x = {"fsdp": f_place + 1 - 2 * side, "tp": t_place}
    over_y = {"fsdp": f_place, "tp": t_place + 2 - 4 * chip}
    over_core = {"fsdp": f_place, "tp": t_place + 1 - 2 * core}
    return side, chip, core, over_x, over_y, over_core


def greet(*others):
    barrier = pltpu.get_barrier_semaphore()
    count = 0
    for other, there in others:
        if there is True:
            pl.semaphore_signal(barrier, inc=1, device_id=other, device_id_type=MESH)
            count = count + 1
        else:

            @pl.when(there)
            def _():
                pl.semaphore_signal(barrier, inc=1, device_id=other, device_id_type=MESH)

            count = count + there.astype(jnp.int32)
    pl.semaphore_wait(barrier, count)


class Copies:
    def __init__(self, send_sems, recv_sems):
        self.send_sems, self.recv_sems, self.count, self.started = send_sems, recv_sems, 0, []

    def remote(self, source, target, device):
        copy = pltpu.make_async_remote_copy(
            src_ref=source,
            dst_ref=target,
            send_sem=self.send_sems.at[self.count],
            recv_sem=self.recv_sems.at[self.count],
            device_id=device,
            device_id_type=MESH,
        )
        self.count += 1
        copy.start()
        self.started.append(copy)
        return copy

    def local(self, source, target):
        copy = pltpu.make_async_copy(source, target, self.send_sems.at[self.count])
        self.count += 1
        copy.start()
        return copy


def half(which, width):
    return pl.ds(pl.multiple_of(which * width, 128), width)


def chain(planes):
    f_place, t_place = lax.axis_index("fsdp"), lax.axis_index("tp")
    plane = f_place // 2
    above = {"fsdp": f_place + 2, "tp": t_place}
    below = {"fsdp": f_place - 2, "tp": t_place}
    return plane, above, below, plane < planes - 1, plane > 0


class PlaneGather:
    def __init__(self, planes, whole, send_sems, recv_sems):
        self.planes, self.whole, self.send_sems, self.recv_sems = planes, whole, send_sems, recv_sems
        self.plane, above, below, has_above, has_below = chain(planes)
        self.side = lax.axis_index("fsdp") % 2
        self.devices, self.has_after = (above, below), (has_above, has_below)

    def spot(self, plane, piece):
        return self.whole.at[plane, self.side if piece == 0 else 1 - self.side]

    def copy(self, way, step, piece, back):
        ref = self.spot(self.plane - back if way == 0 else self.plane + back, piece)
        return pltpu.make_async_remote_copy(
            src_ref=ref,
            dst_ref=ref,
            send_sem=self.send_sems.at[way, step, piece],
            recv_sem=self.recv_sems.at[way, step, piece],
            device_id=self.devices[way],
            device_id_type=MESH,
        )

    def exists(self, way, back):
        return self.plane >= back if way == 0 else self.plane + back < self.planes

    def send(self, step, piece):
        for way in range(2):

            @pl.when(self.has_after[way] & self.exists(way, step - 1))
            def _():
                self.copy(way, step, piece, step - 1).start()

    def receive(self, step, piece):
        for way in range(2):

            @pl.when(self.exists(way, step))
            def _():
                self.copy(way, step, piece, step).wait_recv()

    def drain(self):
        for step in range(1, self.planes):
            for piece in range(2):
                for way in range(2):

                    @pl.when(self.has_after[way] & self.exists(way, step - 1))
                    def _():
                        self.copy(way, step, piece, step - 1).wait_send()


def gather_kernel(
    planes,
    input_ref,
    segment_ref,
    gain_ref,
    bias_ref,
    w_out_ref,
    w_fc2_ref,
    given_ref,
    qkv_ref,
    fc1_ref,
    normed_all,
    given_all,
    qo_all,
    head_all,
    fc1_block,
    fc2_kept_ref,
    fc2_going_ref,
    bound_ref,
    cos_ref,
    sin_ref,
    normed_ref,
    out_ref,
    send_sems,
    recv_sems,
    plane_send_sems,
    plane_recv_sems,
    head_send_sems,
    head_recv_sems,
):
    side, chip, core, over_x, over_y, over_core = neighbours()
    plane, above, below, has_above, has_below = chain(planes)
    rows = input_ref.shape[0]
    cut = rows // 2
    length = segment_ref.shape[1]
    out_ref[...] = w_out_ref[...].T
    zeros = length - jnp.sum(segment_ref[...], axis=1, keepdims=True)
    bound_ref[side] = jnp.broadcast_to(zeros.astype(wide), bound_ref.shape[1:])
    greet(
        (over_x, True), (over_y, True), (over_core, True), (above, has_above), (below, has_below)
    )
    copies = Copies(send_sems, recv_sems)

    width = out_ref.shape[1] // 2
    qo = PlaneGather(planes, qo_all, plane_send_sems, plane_recv_sems)
    qo_kept, qo_came = [], []
    for part in range(4):
        source = qkv_ref.at[part] if part < 3 else out_ref
        target = qo_all.at[plane, side, :, pl.ds(part * width, width)]
        qo_kept.append(copies.local(source.at[:, half(side, width)], target))
        qo_came.append(copies.remote(source.at[:, half(1 - side, width)], target, over_x))
    bounds = copies.remote(bound_ref.at[side], bound_ref.at[side], over_x)
    mine = [whole.at[side, chip, core] for whole in (normed_all, given_all)]
    y_slot = [whole.at[side, 1 - chip, core] for whole in (normed_all, given_all)]
    x_slot = [whole.at[1 - side, chip, core] for whole in (normed_all, given_all)]
    y_given = copies.remote(given_ref, mine[1], over_y)
    for copy in qo_kept:
        copy.wait()
    qo.send(1, 0)

    tokens = input_ref[...].astype(wide)
    normed_ref[...] = layer_norm(
        tokens, gain_ref[...].astype(wide), bias_ref[...].astype(wide)
    ).astype(narrow)
    kept = [copies.local(normed_ref, mine[0]), copies.local(given_ref, mine[1])]
    last = [
        copies.remote(normed_ref, mine[0], over_core),
        copies.remote(given_ref, mine[1], over_core),
    ]
    ff_width, head_width = fc1_ref.shape[1] // 2, head_all.shape[3]
    head = PlaneGather(planes, head_all, head_send_sems, head_recv_sems)

    def fc1_head(which):
        return fc1_ref.at[:, pl.ds(pl.multiple_of(which * ff_width, 128), head_width)]

    def fc1_tail(which):
        start = pl.multiple_of(which * ff_width + head_width, 128)
        return fc1_ref.at[:, pl.ds(start, ff_width - head_width)]

    head_kept = copies.local(fc1_head(side), head_all.at[plane, side])
    kept.append(copies.local(fc1_tail(side), fc1_block.at[side]))
    for copy in qo_came:
        copy.wait_recv()
    qo.send(1, 1)
    x_normed = copies.remote(normed_ref, mine[0], over_x)
    y_normed = copies.remote(normed_ref, mine[0], over_y)
    head_came = copies.remote(fc1_head(1 - side), head_all.at[plane, side], over_x)

    def forward(gather, step, piece):
        gather.receive(step - 1, piece)
        gather.send(step, piece)

    if planes > 2:
        forward(qo, 2, 0)
    bounds.wait_recv()
    step = min(256, length)
    frequency, sign = lane_constants()

    def tables(i, carry):
        here = pl.ds(pl.multiple_of(i * step, 8), step)
        sequence, first = i // (length // step), (i % (length // step)) * step
        place = (first + lax.broadcasted_iota(jnp.int32, (step, 1), 0)).astype(wide)
        bound = bound_ref[sequence, 0:1, 0:1]
        angles = (place - jnp.where(place >= bound, bound, 0.0)) * frequency
        cos_ref[here] = jnp.cos(angles)
        sin_ref[here] = jnp.sin(angles) * sign
        return carry

    lax.fori_loop(0, 2 * length // step, tables, 0)
    if planes > 2:
        forward(qo, 2, 1)
    ff_rows = w_fc2_ref.shape[0] // 2
    for target, which in ((fc2_kept_ref, side), (fc2_going_ref, 1 - side)):
        target[...] = w_fc2_ref[pl.ds(pl.multiple_of(which * ff_rows, 128), ff_rows)].T
    if planes > 3:
        forward(qo, 3, 0)
    x_normed.wait_recv()
    x_given = copies.remote(given_ref, mine[1], over_x)
    corner = [[copies.remote(x_slot[0], x_slot[0], over_y)]]
    last.append(copies.remote(x_slot[0], x_slot[0], over_core))
    if planes > 3:
        forward(qo, 3, 1)
    for k in range(4, planes):
        for piece in range(2):
            forward(qo, k, piece)
    head_kept.wait()
    head.send(1, 0)
    head_came.wait_recv()
    head.send(1, 1)
    y_given.wait_recv()
    last.append(copies.remote(y_slot[1], y_slot[1], over_core))
    y_normed.wait_recv()
    last.append(copies.remote(y_slot[0], y_slot[0], over_core))
    x_given.wait_recv()
    part = y_slot[1].at[pl.ds(0, cut)]
    other_part = x_slot[1].at[pl.ds(cut, rows - cut)]
    corner.append([copies.remote(part, part, over_x), copies.remote(other_part, other_part, over_y)])
    last.append(copies.remote(fc1_tail(1 - side), fc1_block.at[side], over_x))
    last.append(copies.remote(x_slot[1], x_slot[1], over_core))
    for k in range(2, planes):
        for piece in range(2):
            forward(head, k, piece)
    for whole, parts in zip((normed_all, given_all), corner):
        for copy in parts:
            copy.wait_recv()
        slot = whole.at[1 - side, 1 - chip, core]
        last.append(copies.remote(slot, slot, over_core))
    for piece in range(2):
        qo.receive(planes - 1, piece)
        head.receive(planes - 1, piece)
    for copy in kept:
        copy.wait()
    for copy in copies.started:
        copy.wait_send()
    qo.drain()
    head.drain()
    for copy in last:
        copy.wait_recv()


def gather_tokens(planes, inputs, segments, gain, bias, given, w_qkv, w_out, fc1, w_fc2):
    mine, rows, lanes = inputs.shape[0], fc1.shape[0], 2 * HEAD_DIM
    tokens, length = 8 * mine, segments.shape[1]
    columns = 2 * w_out.shape[0]
    whole = jax.ShapeDtypeStruct((2, 2, 2, mine, D), narrow)
    head = max(128, fc1.shape[1] // 8)
    block = jax.ShapeDtypeStruct((2, rows, fc1.shape[1] // 2 - head), narrow)
    table = jax.ShapeDtypeStruct((2 * length, lanes), wide)
    weights = jax.ShapeDtypeStruct((planes, 2, rows, columns), narrow)
    anywhere, vmem = pl.BlockSpec(memory_space=pl.ANY), pl.BlockSpec(memory_space=pltpu.VMEM)
    ff_half = jax.ShapeDtypeStruct((rows, w_fc2.shape[0] // 2), narrow)
    outs = pl.pallas_call(
        functools.partial(gather_kernel, planes),
        in_specs=[vmem] * 6 + [anywhere] * 3,
        out_specs=[anywhere] * 5 + [vmem] * 5,
        out_shape=[
            whole,
            whole,
            weights,
            jax.ShapeDtypeStruct((planes, 2, rows, head), narrow),
            block,
            ff_half,
            ff_half,
            jax.ShapeDtypeStruct((2, 8, 128), wide),
            table,
            table,
        ],
        scratch_shapes=[
            pltpu.VMEM((mine, D), narrow),
            pltpu.VMEM((rows, w_out.shape[0]), narrow),
            pltpu.SemaphoreType.DMA((32,)),
            pltpu.SemaphoreType.DMA((32,)),
            pltpu.SemaphoreType.DMA((2, planes, 2)),
            pltpu.SemaphoreType.DMA((2, planes, 2)),
            pltpu.SemaphoreType.DMA((2, planes, 2)),
            pltpu.SemaphoreType.DMA((2, planes, 2)),
        ],
        compiler_params=pltpu.CompilerParams(
            collective_id=1, has_side_effects=True, vmem_limit_bytes=VMEM
        ),
        name="gather_tokens",
    )(inputs, segments, gain, bias, w_out, w_fc2, given, w_qkv, fc1)
    normed_all, given_all, qo_all, head_all = outs[:4]
    return (
        normed_all.reshape(tokens, D),
        given_all.reshape(tokens, D),
        qo_all.reshape(D, columns),
        head_all.reshape(D, head),
    ) + tuple(outs[4:])


def scatter_kernel(planes, which, *refs):
    lefts = sorted(set(which))
    n_left, n_right = len(lefts), len(which)
    left_refs, right_refs = refs[:n_left], refs[n_left : n_left + n_right]
    (
        fc1_head_ref,
        fc1_tail_ref,
        bias_ref,
        kept_ref,
        came_ref,
        out_ref,
        weight_all,
        active_all,
        slope_all,
        grad_all,
        left_vmem,
        own,
        turned,
        going,
        came,
        active_stage,
        slope_stage,
        grad_stage,
        load_sems,
        send_sems,
        recv_sems,
        store_sems,
    ) = refs[n_left + n_right :]
    side = lax.axis_index("fsdp") % 2
    plane, above, below, has_above, has_below = chain(planes)
    devices, has_after, has_before = (above, below), (has_above, has_below), (has_below, has_above)
    group, width = own.shape[1], right_refs[0].shape[1]
    rows, tokens = group // 2, right_refs[0].shape[0]

    def load(j):
        return [
            pltpu.make_async_copy(
                left_refs[i].at[:, pl.ds(pl.multiple_of(j * group, 128), group)],
                left_vmem.at[i, j],
                load_sems.at[i, j],
            )
            for i in range(n_left)
        ]

    def order(k):
        return jnp.where(plane < planes // 2, planes - 1 - k, k)

    for k in range(planes):
        for copy in load(order(k)):
            copy.start()
    greet((above, has_above), (below, has_below))
    own_weight = [
        pltpu.make_async_copy(ref, weight_all.at[plane, at], store_sems.at[3, piece])
        for piece, (ref, at) in enumerate(((kept_ref, side), (came_ref, 1 - side)))
    ]

    def depth(way):
        return plane if way == 0 else planes - 1 - plane

    def named(way, block):
        return block if way == 0 else planes - 1 - block

    def is_weight(at, number):
        return number <= at + 1

    def weight_block(at, number):
        return at - number + 1

    def sum_block(at, number):
        return planes + 1 + at - number

    def weight_copy(way, number, at, piece):
        j = named(way, weight_block(at, number))
        ref = weight_all.at[j, side if piece == 0 else 1 - side]
        return pltpu.make_async_remote_copy(
            src_ref=(kept_ref, came_ref)[piece] if number == 1 else ref,
            dst_ref=ref,
            send_sem=send_sems.at[way, number, piece],
            recv_sem=recv_sems.at[way, number, piece],
            device_id=devices[way],
            device_id_type=MESH,
        )

    cut = own.shape[0] // 2
    spans = (slice(0, cut), slice(cut, 2 * cut))

    def sum_copy(way, number, at, receiver, arriving, piece):
        j = named(way, sum_block(at, number))
        spot = j if way == 0 else jnp.where(j == receiver, planes, j)
        here = pl.ds(piece * cut, cut)
        return j, spot, pltpu.make_async_remote_copy(
            src_ref=came.at[spot, here] if arriving else going.at[j, here],
            dst_ref=came.at[spot, here],
            send_sem=send_sems.at[way, number, 2 + piece],
            recv_sem=recv_sems.at[way, number, 2 + piece],
            device_id=devices[way],
            device_id_type=MESH,
        )

    def next_plane(way):
        return plane + 1 if way == 0 else plane - 1

    def finish_send(way, number, piece):
        at = depth(way)

        @pl.when(has_after[way] & is_weight(at, number))
        def _():
            weight_copy(way, number, at, piece).wait_send()

        @pl.when(has_after[way] & jnp.logical_not(is_weight(at, number)))
        def _():
            sum_copy(way, number, at, next_plane(way), False, piece)[2].wait_send()

    def take(way, number, piece):
        at = depth(way) - 1

        @pl.when(has_before[way] & is_weight(at, number))
        def _():
            weight_copy(way, number, at, piece).wait_recv()

        @pl.when(has_before[way] & jnp.logical_not(is_weight(at, number)))
        def _():
            j, spot, copy = sum_copy(way, number, at, plane, True, piece)
            copy.wait_recv()
            here = spans[piece]

            @pl.when(j == plane)
            def _():
                own[here] += came[spot, here].astype(wide)

            @pl.when(j != plane)
            def _():
                going[j, here] = (
                    going[j, here].astype(wide) + came[spot, here].astype(wide)
                ).astype(narrow)

    def give(way, number, piece):
        at = depth(way)

        @pl.when(has_after[way] & is_weight(at, number))
        def _():
            weight_copy(way, number, at, piece).start()

        @pl.when(has_after[way] & jnp.logical_not(is_weight(at, number)))
        def _():
            sum_copy(way, number, at, next_plane(way), False, piece)[2].start()

    step = slope_stage.shape[1]
    blocks = tokens // step

    def turn(i, carry):
        here = pl.ds(pl.multiple_of(i * step, 128), step)
        for number, right_ref in enumerate(right_refs):
            turned[number * width : (number + 1) * width, here] = right_ref[here].T
        return carry

    def multiply(k):
        j = order(k)
        for copy in load(j):
            copy.wait()
        for i in range(n_left):
            numbers = [number for number, left in enumerate(which) if left == lefts[i]]
            here = slice(numbers[0] * width, (numbers[-1] + 1) * width)
            block = nn(turned[here], left_vmem[i, j])
            going[j, here] = block.astype(narrow)

            @pl.when(j == plane)
            def _():
                own[here] = block

    def store_hidden(i, slot):
        here = pl.ds(pl.multiple_of(i * step, 16), step)
        return [
            pltpu.make_async_copy(slope_stage.at[slot], slope_all.at[here], store_sems.at[0, slot]),
            pltpu.make_async_copy(active_stage.at[slot], active_all.at[here], store_sems.at[1, slot]),
        ]

    def hidden_units(i, carry):
        here = pl.ds(pl.multiple_of(i * step, 128), step)
        slot = i % 2
        parts = []
        for part_ref in (fc1_head_ref, fc1_tail_ref):
            part = nn(left_vmem[0, 0, here], part_ref[0:group])
            for j in range(1, planes):
                part += nn(left_vmem[0, j, here], part_ref[j * group : (j + 1) * group])
            parts.append(part)
        hidden = bias_ref[...] + jnp.concatenate(parts, axis=1)
        squared = hidden * hidden
        inner = jnp.tanh(0.7978845608028654 * hidden * (1.0 + 0.044715 * squared))
        half_sum = 0.5 * (1.0 + inner)
        active = (hidden * half_sum).astype(narrow)

        @pl.when(i >= 2)
        def _():
            for copy in store_hidden(i - 2, slot):
                copy.wait()

        active_stage[slot] = active
        slope_stage[slot] = half_sum + hidden * (0.5 * (1.0 - inner * inner)) * (
            0.7978845608028654 * (1.0 + 3.0 * 0.044715 * squared)
        )
        for copy in store_hidden(i, slot):
            copy.start()
        turned[:, here] = active.T
        return carry

    def store_grad(j, slot):
        return pltpu.make_async_copy(grad_stage.at[slot], grad_all.at[j], store_sems.at[2, slot])

    def fc2_gradient(j, carry):
        slot = j % 2

        @pl.when(j >= 2)
        def _():
            store_grad(j - 2, slot).wait()

        block = nn(turned[...], left_vmem[n_left - 1, j]).astype(narrow)
        for number in range(2):
            grad_stage[slot, number] = block[:, number * rows : (number + 1) * rows]
        store_grad(j, slot).start()
        return carry

    for piece in range(2):
        for way in range(2):
            give(way, 1, piece)
    for copy in own_weight:
        copy.start()
    lax.fori_loop(0, blocks, turn, 0)
    multiply(0)
    multiply(1)

    work = [lambda: [multiply(k) for k in range(2, planes)]]
    parts = min(4, blocks)
    for part in range(parts):
        work.append(
            functools.partial(
                lax.fori_loop, part * blocks // parts, (part + 1) * blocks // parts, hidden_units, 0
            )
        )
    for part in range(2):
        work.append(
            functools.partial(
                lax.fori_loop, part * planes // 2, (part + 1) * planes // 2, fc2_gradient, 0
            )
        )
    for number in range(2, planes + 1):
        for piece in range(2):
            for way in range(2):
                take(way, number - 1, piece)
                finish_send(way, number - 1, piece)
                give(way, number, piece)
            if work:
                work.pop(0)()
    for part in work:
        part()
    for piece in range(2):
        for way in range(2):
            take(way, planes, piece)
    for number in range(2):
        out_ref[number] = own[:, number * rows : (number + 1) * rows].astype(narrow)
    for piece in range(2):
        for way in range(2):
            finish_send(way, planes, piece)
    for slot in range(2):
        for copy in store_hidden(blocks - 2 + slot, slot) + [store_grad(planes - 2 + slot, slot)]:
            copy.wait()
    for copy in own_weight:
        copy.wait()


def backward_step(planes, lefts, rights, which, fc1, bias, weight, collective_id):
    tokens, width = rights[0].shape
    group, columns, hidden = D // planes, width * len(rights), bias.shape[1]
    rows, step = group // 2, min(256, tokens // 2)
    anywhere, vmem = pl.BlockSpec(memory_space=pl.ANY), pl.BlockSpec(memory_space=pltpu.VMEM)
    total, weight_all, active, slope, grad = pl.pallas_call(
        functools.partial(scatter_kernel, planes, which),
        in_specs=[anywhere] * len(lefts) + [vmem] * (len(rights) + 3) + [anywhere] * 2,
        out_specs=[vmem] + [anywhere] * 4,
        out_shape=[
            jax.ShapeDtypeStruct((2, columns, rows), narrow),
            jax.ShapeDtypeStruct((planes, 2, rows, weight[0].shape[1]), narrow),
            jax.ShapeDtypeStruct((tokens, hidden), narrow),
            jax.ShapeDtypeStruct((tokens, hidden), wide),
            jax.ShapeDtypeStruct((planes, 2, hidden, rows), narrow),
        ],
        scratch_shapes=[
            pltpu.VMEM((len(lefts), planes, tokens, group), narrow),
            pltpu.VMEM((columns, group), wide),
            pltpu.VMEM((columns, tokens), narrow),
            pltpu.VMEM((planes, columns, group), narrow),
            pltpu.VMEM((planes + 1, columns, group), narrow),
            pltpu.VMEM((2, step, hidden), narrow),
            pltpu.VMEM((2, step, hidden), wide),
            pltpu.VMEM((2, 2, hidden, rows), narrow),
            pltpu.SemaphoreType.DMA((len(lefts), planes)),
            pltpu.SemaphoreType.DMA((2, planes + 1, 4)),
            pltpu.SemaphoreType.DMA((2, planes + 1, 4)),
            pltpu.SemaphoreType.DMA((4, 2)),
        ],
        compiler_params=pltpu.CompilerParams(
            collective_id=collective_id, has_side_effects=True, vmem_limit_bytes=VMEM
        ),
        cost_estimate=pl.CostEstimate(
            flops=40 * tokens * D * columns, bytes_accessed=2 * tokens * D, transcendentals=0
        ),
        name="backward_step",
    )(*lefts, *rights, *fc1, bias, *weight)
    return total, weight_all.reshape(D, weight[0].shape[1]), active, slope, grad


def project_kernel(normed_ref, given_ref, in_ref, out_ref, bias_ref, projected_ref, given_attn_ref):
    projected_ref[...] = nn(normed_ref[...], in_ref[...]) + bias_ref[...]
    given_attn_ref[...] = nn(given_ref[...], out_ref[...]).astype(narrow)


def project(normed, given, weights, bias):
    tokens, width = normed.shape[0], weights.shape[1] // 4
    block = min(256, tokens)
    row = pl.BlockSpec((block, D), lambda i: (i, 0))
    return pl.pallas_call(
        project_kernel,
        grid=(tokens // block,),
        in_specs=[
            row,
            row,
            pl.BlockSpec((D, 3 * width), lambda i: (0, 0)),
            pl.BlockSpec((D, width), lambda i: (0, 3)),
            pl.BlockSpec((1, 3 * width), lambda i: (0, 0)),
        ],
        out_specs=[
            pl.BlockSpec((block, 3 * width), lambda i: (i, 0)),
            pl.BlockSpec((block, width), lambda i: (i, 0)),
        ],
        out_shape=[
            jax.ShapeDtypeStruct((tokens, 3 * width), wide),
            jax.ShapeDtypeStruct((tokens, width), narrow),
        ],
        compiler_params=pltpu.CompilerParams(vmem_limit_bytes=VMEM),
        cost_estimate=pl.CostEstimate(
            flops=8 * tokens * D * width, bytes_accessed=8 * tokens * D, transcendentals=0
        ),
        name="project",
    )(normed, given, weights, weights, bias)


def reduce_kernel(terms, n_left, n_right, *refs):
    left_refs, right_refs = refs[:n_left], refs[n_left : n_left + n_right]
    (
        extra_ref,
        out_ref,
        extra_came,
        core_going,
        core_came,
        sums,
        x_going,
        x_came,
        y_going,
        y_came,
        send_sems,
        recv_sems,
    ) = refs[n_left + n_right :]
    side, chip, core, over_x, over_y, over_core = neighbours()
    mine, columns = out_ref.shape
    cut = columns // 4
    first, second = slice(0, cut), slice(cut, columns)
    greet((over_x, True), (over_y, True), (over_core, True))

    extra = pltpu.make_async_remote_copy(
        src_ref=extra_ref.at[1 - side],
        dst_ref=extra_came,
        send_sem=send_sems.at[0, 4],
        recv_sem=recv_sems.at[0, 4],
        device_id=over_x,
        device_id_type=MESH,
    )
    extra.start()

    def copy(lane, number):
        going, came, other = (
            (core_going, core_came, over_core),
            (x_going, x_came, over_x),
            (y_going, y_came, over_y),
        )[lane]
        if lane == 0:
            here = number
        else:
            here = (number, slice(None), first if (lane == 1) == (number < 2) else second)
        return pltpu.make_async_remote_copy(
            src_ref=going.at[here],
            dst_ref=came.at[here],
            send_sem=send_sems.at[lane, number],
            recv_sem=recv_sems.at[lane, number],
            device_id=other,
            device_id_type=MESH,
        )

    def product(number):
        here = pl.ds(pl.multiple_of(number * mine, 16), mine)
        total = None
        for left, start, width, right, column in terms:
            part = nt(
                left_refs[left][here, start : start + width],
                right_refs[right][:, column : column + width],
            )
            total = part if total is None else total + part
        return total

    def quarter(q, carry):
        its_side = jnp.where(q < 2, 1 - side, side)
        its_chip = jnp.where(q % 2 == 0, 1 - chip, chip)
        base = (its_side * 2 + its_chip) * 2
        core_going[q] = product(base + 1 - core).astype(narrow)
        copy(0, q).start()
        block = product(base + core)
        copy(0, q).wait_recv()
        sums[q] = block + core_came[q].astype(wide)

        for number in range(2):

            @pl.when(q == number)
            def _():
                x_going[number, :, first] = sums[number, :, first].astype(narrow)
                copy(1, number).start()

            @pl.when(q == 2 * number)
            def _():
                y_going[number, :, second] = sums[2 * number, :, second].astype(narrow)
                copy(2, number).start()

        return carry

    lax.fori_loop(0, 4, quarter, 0)
    copy(1, 0).wait_recv()
    y_going[2, :, first] = (sums[2, :, first] + x_came[0, :, first].astype(wide)).astype(narrow)
    copy(2, 2).start()
    copy(2, 0).wait_recv()
    x_going[2, :, second] = (sums[1, :, second] + y_came[0, :, second].astype(wide)).astype(narrow)
    copy(1, 2).start()
    copy(1, 1).wait_recv()
    out_ref[:, first] = sums[3, :, first] + x_came[1, :, first].astype(wide)
    copy(2, 1).wait_recv()
    out_ref[:, second] = sums[3, :, second] + y_came[1, :, second].astype(wide)
    copy(2, 2).wait_recv()
    out_ref[:, first] += y_came[2, :, first].astype(wide)
    copy(1, 2).wait_recv()
    out_ref[:, second] += x_came[2, :, second].astype(wide)
    extra.wait()
    for q in range(4):
        copy(0, q).wait_send()
    for lane in (1, 2):
        for number in range(3):
            copy(lane, number).wait_send()


def distinct(values):
    kept = []
    for value in values:
        if not any(value is other for other in kept):
            kept.append(value)
    return kept


def place_of(value, values):
    return next(i for i, other in enumerate(values) if other is value)


def reduce_products(mine, terms, extra, collective_id):
    lefts = distinct([term[0] for term in terms])
    rights = distinct([term[3] for term in terms])
    places = tuple(
        (place_of(a, lefts), start, width, place_of(w, rights), column)
        for a, start, width, w, column in terms
    )
    tokens, depth = terms[0][0].shape[0], sum(term[2] for term in terms)
    anywhere, vmem = pl.BlockSpec(memory_space=pl.ANY), pl.BlockSpec(memory_space=pltpu.VMEM)
    return pl.pallas_call(
        functools.partial(reduce_kernel, places, len(lefts), len(rights)),
        in_specs=[vmem] * (len(lefts) + len(rights)) + [anywhere],
        out_specs=[vmem, anywhere],
        out_shape=[
            jax.ShapeDtypeStruct((mine, D), wide),
            jax.ShapeDtypeStruct(extra.shape[1:], extra.dtype),
        ],
        scratch_shapes=[
            pltpu.VMEM((4, mine, D), narrow),
            pltpu.VMEM((4, mine, D), narrow),
            pltpu.VMEM((4, mine, D), wide),
            pltpu.VMEM((3, mine, D), narrow),
            pltpu.VMEM((3, mine, D), narrow),
            pltpu.VMEM((3, mine, D), narrow),
            pltpu.VMEM((3, mine, D), narrow),
            pltpu.SemaphoreType.DMA((3, 5)),
            pltpu.SemaphoreType.DMA((3, 5)),
        ],
        compiler_params=pltpu.CompilerParams(
            collective_id=collective_id, has_side_effects=True, vmem_limit_bytes=VMEM
        ),
        cost_estimate=pl.CostEstimate(
            flops=8 * tokens * depth * D, bytes_accessed=2 * depth * (tokens + D), transcendentals=0
        ),
        name="reduce_products",
    )(*lefts, *rights, extra)


def solution(mesh):
    nf = mesh.shape["fsdp"]
    nt_axis = mesh.shape["tp"]
    columns_of_planes = [list(range(side, nf, 2)) for side in range(2)]
    swap_f = [(f, f ^ 1) for f in range(nf)]
    swap_core = [(t, t ^ 1) for t in range(nt_axis)]
    swap_chip = [(t, t ^ 2) for t in range(nt_axis)]

    def send_x(v):
        return lax.ppermute(v, "fsdp", swap_f)

    def send_y(v):
        return lax.ppermute(v, "tp", swap_chip)

    def send_core(v):
        return lax.ppermute(v, "tp", swap_core)

    def gather_planes(block):
        block = block.reshape(block.shape[0] * block.shape[1], block.shape[2])
        return lax.all_gather(
            block, "fsdp", axis=0, tiled=True, axis_index_groups=columns_of_planes
        )

    def local(
        inputs,
        segments,
        ln_gain,
        ln_bias,
        w_qkv,
        b_qkv,
        w_out,
        b_out,
        w_fc1,
        b_fc1,
        w_fc2,
        b_fc2,
        cotangent,
    ):
        f_place = lax.axis_index("fsdp")
        t_place = lax.axis_index("tp")
        side = f_place % 2
        chip, core = t_place // 2, t_place % 2
        length = segments.shape[1]
        mine = inputs.shape[0]
        rows = w_fc1.shape[0]
        half_qkv, half_ff = w_qkv.shape[2] // 2, w_fc1.shape[1] // 2

        def pick(v, index, axis=0):
            return lax.dynamic_index_in_dim(v, index, axis, keepdims=False)

        def in_order(kept, came):
            return jnp.where(side == 0, jnp.stack([kept, came]), jnp.stack([came, kept]))

        def sum_planes(grads):
            return lax.psum_scatter(
                grads.astype(narrow),
                "fsdp",
                scatter_dimension=0,
                tiled=True,
                axis_index_groups=columns_of_planes,
            )

        def halves_of(kept, came):
            return in_order(kept, came).astype(wide)

        def reduce_all(v):
            for axis, size in (("tp", nt_axis), ("fsdp", nf)):
                bit = 1
                while bit < size:
                    v = v + lax.ppermute(v, axis, [(i, i ^ bit) for i in range(size)])
                    bit *= 2
            return v

        (
            normed,
            grad_rows,
            full_qo,
            fc1_head,
            fc1_block,
            fc2_kept,
            fc2_going,
            bounds,
            cosine,
            sine,
        ) = gather_tokens(
            nf // 2,
            inputs,
            segments,
            ln_gain.reshape(1, D),
            ln_bias.reshape(1, D),
            cotangent,
            w_qkv,
            w_out,
            w_fc1,
            w_fc2,
        )
        fc1_tail = gather_planes(fc1_block)
        fc2_came = send_x(fc2_going)
        tokens_in = inputs.astype(wide)
        _, norm_back = jax.vjp(
            layer_norm, tokens_in, ln_gain.astype(wide), ln_bias.astype(wide)
        )

        bias_qkv = lax.dynamic_slice_in_dim(b_qkv, side * half_qkv, half_qkv, axis=1)
        bias_fc1 = lax.dynamic_slice_in_dim(b_fc1, side * half_ff, half_ff, axis=0)

        projected, grad_mixed = project(
            normed, grad_rows, full_qo, bias_qkv.astype(wide).reshape(1, 3 * half_qkv)
        )
        mixed, grad_q, grad_k, grad_v = attention(
            bounds, cosine, sine, projected, grad_mixed, length
        )
        sum_qo, full_fc2, active_low, slope, grad_w2 = backward_step(
            nf // 2,
            [normed, grad_rows],
            [grad_q, grad_k, grad_v, mixed],
            (0, 0, 0, 1),
            (fc1_head, fc1_tail),
            bias_fc1.astype(wide).reshape(1, half_ff),
            (fc2_kept, fc2_came),
            2,
        )
        grad_q, grad_k, grad_v, sum_qo = lax.optimization_barrier((grad_q, grad_k, grad_v, sum_qo))
        total_fc2 = sum_planes(grad_w2.reshape(-1, rows))
        grad_hidden = (nn(grad_rows, full_fc2) * slope).astype(narrow)
        grad_w1 = tn(normed, grad_hidden).astype(narrow)
        mixed, grad_w1 = lax.optimization_barrier((mixed, grad_w1))
        branch_local, came_qo = reduce_products(
            mine,
            [(mixed, 0, half_qkv, full_qo, 3 * half_qkv), (active_low, 0, half_ff, full_fc2, 0)],
            sum_qo,
            4,
        )
        total_fc2, grad_hidden, grad_w1, branch_local = lax.optimization_barrier(
            (total_fc2, grad_hidden, grad_w1, branch_local)
        )
        total_fc1 = sum_planes(grad_w1)
        total_fc2 = total_fc2.reshape(2, half_ff, rows)
        head = fc1_head.shape[1]
        grad_normed, came_fc2 = reduce_products(
            mine,
            [
                (grad_q, 0, half_qkv, full_qo, 0),
                (grad_k, 0, half_qkv, full_qo, half_qkv),
                (grad_v, 0, half_qkv, full_qo, 2 * half_qkv),
                (grad_hidden, 0, head, fc1_head, 0),
                (grad_hidden, head, half_ff - head, fc1_tail, 0),
            ],
            total_fc2,
            3,
        )
        sum_qo = halves_of(pick(sum_qo, side), came_qo)
        sum_fc2 = halves_of(pick(total_fc2, side), came_fc2)
        grad_projected = jnp.concatenate([grad_q, grad_k, grad_v], axis=1)
        outputs = (tokens_in + branch_local + b_out.astype(wide) + b_fc2.astype(wide)).astype(narrow)
        grad_tokens, grad_gain, grad_offset = norm_back(grad_normed)
        grad_tokens = grad_tokens + cotangent.astype(wide)

        grad_w_qkv = sum_qo[:, : 3 * half_qkv].reshape(2, 3, half_qkv, rows)
        grad_w_qkv = grad_w_qkv.transpose(1, 3, 0, 2).reshape(3, rows, 2 * half_qkv)
        grad_w_out = sum_qo[:, 3 * half_qkv :].reshape(2 * half_qkv, rows)
        grad_w_fc2 = sum_fc2.reshape(2 * half_ff, rows)

        anchor = jnp.zeros((), jnp.int32)
        bias_qkv_full = lax.dynamic_update_slice(
            jnp.zeros((3, D), wide),
            jnp.sum(grad_projected.astype(wide), axis=0).reshape(3, half_qkv),
            (anchor, (2 * t_place + side) * half_qkv),
        )
        bias_fc1_full = lax.dynamic_update_slice(
            jnp.zeros((FF,), wide),
            jnp.sum(grad_hidden.astype(wide), axis=0),
            ((2 * t_place + side) * half_ff,),
        )
        cotangent_sum = jnp.sum(cotangent.astype(wide), axis=0)
        small = reduce_all(
            jnp.concatenate(
                [bias_qkv_full.reshape(-1), bias_fc1_full, grad_gain, grad_offset, cotangent_sum]
            ).reshape(-1, 128)
        ).reshape(-1)
        total_fc1, outputs, grad_tokens, grad_w_qkv, grad_w_out, grad_w_fc2 = (
            lax.optimization_barrier(
                (total_fc1, outputs, grad_tokens, grad_w_qkv, grad_w_out, grad_w_fc2)
            )
        )
        parts = total_fc1.reshape(2, rows, total_fc1.shape[1])
        kept, came = pick(parts, side).astype(wide), send_x(pick(parts, 1 - side)).astype(wide)
        grad_w_fc1 = jnp.where(
            side == 0,
            jnp.concatenate([kept, came], axis=1),
            jnp.concatenate([came, kept], axis=1),
        )
        total_qkv = small[: 3 * D].reshape(3, D)
        total_b_fc1 = small[3 * D : 3 * D + FF]
        total_gain, total_offset, total_out = small[3 * D + FF :].reshape(3, D)
        return (
            outputs,
            grad_tokens,
            total_gain,
            total_offset,
            grad_w_qkv,
            total_qkv,
            grad_w_out,
            total_out,
            grad_w_fc1,
            total_b_fc1,
            grad_w_fc2,
            total_out,
        )

    return jax.shard_map(
        local,
        mesh=mesh,
        in_specs=(
            P(("fsdp", "tp"), None),
            P("fsdp", None),
            P(),
            P(),
            P(None, "fsdp", "tp"),
            P(None, "tp"),
            P("tp", "fsdp"),
            P(),
            P("fsdp", "tp"),
            P("tp"),
            P("tp", "fsdp"),
            P(),
            P(("fsdp", "tp"), None),
        ),
        out_specs=(
            P(("fsdp", "tp"), None),
            P(("fsdp", "tp"), None),
            P(),
            P(),
            P(None, "fsdp", "tp"),
            P(),
            P("tp", "fsdp"),
            P(),
            P("fsdp", "tp"),
            P(),
            P("tp", "fsdp"),
            P(),
        ),
        check_vma=False,
    )
```

```python
import functools
import math

import jax
import jax.numpy as jnp
from jax import lax
from jax.experimental import pallas as pl
from jax.experimental.pallas import tpu as pltpu
from jax.sharding import PartitionSpec as P

D = 2048
HEAD_DIM = 64
ROT = 32
FF = 8192
VMEM = 62 << 20

wide = jnp.float32
narrow = jnp.bfloat16
norm_epsilon = 1e-05
masked_score = -1e30


def gelu_tanh(values):
    return (
        0.5
        * values
        * (1.0 + jnp.tanh(0.7978845608028654 * (values + 0.044715 * values * values * values)))
    )


def layer_norm(tokens_in, gain, offset):
    centre = jnp.mean(tokens_in, axis=-1, keepdims=True)
    centred = tokens_in - centre
    spread = jnp.mean(centred * centred, axis=-1, keepdims=True)
    return centred * lax.rsqrt(spread + norm_epsilon) * gain + offset


def lane_constants():
    place = lax.broadcasted_iota(jnp.int32, (1, 2 * HEAD_DIM), 1) % HEAD_DIM
    turned = (place % (ROT // 2)).astype(wide) * 2.0
    frequency = jnp.exp(turned * (-math.log(10000.0) / ROT))
    sign = jnp.where(place < ROT // 2, -1.0, 1.0)
    inside = place < ROT
    return jnp.where(inside, frequency, 0.0), jnp.where(inside, sign, 0.0)


def nt(a, b):
    return lax.dot_general(a, b, (((1,), (1,)), ((), ())), preferred_element_type=wide)


def nn(a, b):
    return lax.dot_general(a, b, (((1,), (0,)), ((), ())), preferred_element_type=wide)


def tn(a, b):
    return lax.dot_general(a, b, (((0,), (0,)), ((), ())), preferred_element_type=wide)


def attention_kernel(
    rows,
    bound_ref,
    cos_ref,
    sin_ref,
    q_ref,
    k_ref,
    v_ref,
    do_ref,
    attn_ref,
    gq_ref,
    gk_ref,
    gv_ref,
    kb_ref,
    vb_ref,
    dk_ref,
    dv_ref,
):
    length = q_ref.shape[0]
    lanes = 2 * HEAD_DIM
    place = lax.broadcasted_iota(jnp.int32, (1, lanes), 1)
    low_half = (place % HEAD_DIM) < (ROT // 2)
    scale = HEAD_DIM**-0.5

    def partner(u):
        return jnp.where(
            low_half, pltpu.roll(u, lanes - ROT // 2, 1), pltpu.roll(u, ROT // 2, 1)
        )

    def turn(u, cosine, sine):
        return u * cosine + partner(u) * sine

    def turn_back(u, cosine, sine):
        return u * cosine - partner(u) * sine

    bound = bound_ref[0, 0:1, 0:1].astype(jnp.int32)
    kb_ref[...] = turn(k_ref[...], cos_ref[...], sin_ref[...]).astype(narrow)
    vb_ref[...] = v_ref[...].astype(narrow)
    dk_ref[...] = jnp.zeros_like(dk_ref)
    dv_ref[...] = jnp.zeros_like(dv_ref)
    for first in range(0, length, rows):
        seen = first + rows
        here = slice(first, seen)
        cosine, sine = cos_ref[here], sin_ref[here]
        q_both = (turn(q_ref[here], cosine, sine).astype(narrow) * scale).astype(narrow)
        row_place = first + lax.broadcasted_iota(jnp.int32, (rows, seen), 0)
        key_place = lax.broadcasted_iota(jnp.int32, (rows, seen), 1)
        row_start = first + lax.broadcasted_iota(jnp.int32, (rows, 1), 0)
        opening = jnp.where(row_start >= bound, bound, 0)
        allowed = (key_place <= row_place) & (key_place >= opening)
        cols = [slice(head * HEAD_DIM, (head + 1) * HEAD_DIM) for head in range(2)]
        q = [q_both[:, c] for c in cols]
        k, v = [kb_ref[0:seen, c] for c in cols], [vb_ref[0:seen, c] for c in cols]
        do = [do_ref[here, c] for c in cols]
        scores = [jnp.where(allowed, nt(a, b), masked_score) for a, b in zip(q, k)]
        grad_probs = [nt(a, b) for a, b in zip(do, v)]
        largest = [jnp.max(x, axis=-1, keepdims=True) for x in scores]
        exponent = [jnp.exp(x - m) for x, m in zip(scores, largest)]
        probs = [e * (1.0 / jnp.sum(e, axis=-1, keepdims=True)) for e in exponent]
        probs_low = [p.astype(narrow) for p in probs]
        attn_parts = [nn(p, x) for p, x in zip(probs_low, v)]
        inner = [jnp.sum(p * g, axis=-1, keepdims=True) for p, g in zip(probs, grad_probs)]
        grad_scores = [
            (p * (g - i)).astype(narrow) for p, g, i in zip(probs, grad_probs, inner)
        ]
        dv_parts = [tn(x, p) for x, p in zip(do, probs_low)]
        dq_parts = [nn(g, x) for g, x in zip(grad_scores, k)]
        dk_parts = [tn(x, g) for x, g in zip(q, grad_scores)]
        attn_ref[here] = jnp.concatenate(attn_parts, axis=1).astype(narrow)
        dq = jnp.concatenate(dq_parts, axis=1) * scale
        gq_ref[here] = turn_back(dq, cosine, sine).astype(narrow)
        dk_ref[:, 0:seen] += jnp.concatenate(dk_parts, axis=0)
        dv_ref[:, 0:seen] += jnp.concatenate(dv_parts, axis=0)
    gk_ref[...] = turn_back(dk_ref[...].T, cos_ref[...], sin_ref[...]).astype(narrow)
    gv_ref[...] = dv_ref[...].T.astype(narrow)


def attention(bounds, cosine, sine, projected, grad_attn, length):
    tokens, width = grad_attn.shape
    lanes = 2 * HEAD_DIM
    pairs = width // lanes
    rows = min(512, length)
    bound = pl.BlockSpec((1, 8, 128), lambda s, h: (s, 0, 0))
    table = pl.BlockSpec((length, lanes), lambda s, h: (s, 0))
    block = pl.BlockSpec((length, lanes), lambda s, h: (s, h))
    k_block = pl.BlockSpec((length, lanes), lambda s, h: (s, pairs + h))
    v_block = pl.BlockSpec((length, lanes), lambda s, h: (s, 2 * pairs + h))
    out = jax.ShapeDtypeStruct((tokens, width), narrow)
    return pl.pallas_call(
        functools.partial(attention_kernel, rows),
        grid=(tokens // length, pairs),
        in_specs=[bound, table, table, block, k_block, v_block, block],
        out_specs=[block] * 4,
        out_shape=[out] * 4,
        scratch_shapes=[
            pltpu.VMEM((length, lanes), narrow),
            pltpu.VMEM((length, lanes), narrow),
            pltpu.VMEM((lanes, length), wide),
            pltpu.VMEM((lanes, length), wide),
        ],
        compiler_params=pltpu.CompilerParams(vmem_limit_bytes=VMEM),
        cost_estimate=pl.CostEstimate(
            flops=tokens * length * width * 12, bytes_accessed=tokens * width * 32, transcendentals=0
        ),
        name="attention",
    )(bounds, cosine, sine, projected, projected, projected, grad_attn)


MESH = pl.DeviceIdType.MESH


def neighbours():
    f_place, t_place = lax.axis_index("fsdp"), lax.axis_index("tp")
    side, chip, core = f_place % 2, t_place // 2, t_place % 2
    over_x = {"fsdp": f_place + 1 - 2 * side, "tp": t_place}
    over_y = {"fsdp": f_place, "tp": t_place + 2 - 4 * chip}
    over_core = {"fsdp": f_place, "tp": t_place + 1 - 2 * core}
    return side, chip, core, over_x, over_y, over_core


def greet(*others):
    barrier = pltpu.get_barrier_semaphore()
    count = 0
    for other, there in others:
        if there is True:
            pl.semaphore_signal(barrier, inc=1, device_id=other, device_id_type=MESH)
            count = count + 1
        else:

            @pl.when(there)
            def _():
                pl.semaphore_signal(barrier, inc=1, device_id=other, device_id_type=MESH)

            count = count + there.astype(jnp.int32)
    pl.semaphore_wait(barrier, count)


class Copies:
    def __init__(self, send_sems, recv_sems):
        self.send_sems, self.recv_sems, self.count, self.started = send_sems, recv_sems, 0, []

    def remote(self, source, target, device):
        copy = pltpu.make_async_remote_copy(
            src_ref=source,
            dst_ref=target,
            send_sem=self.send_sems.at[self.count],
            recv_sem=self.recv_sems.at[self.count],
            device_id=device,
            device_id_type=MESH,
        )
        self.count += 1
        copy.start()
        self.started.append(copy)
        return copy

    def local(self, source, target):
        copy = pltpu.make_async_copy(source, target, self.send_sems.at[self.count])
        self.count += 1
        copy.start()
        return copy


def half(which, width):
    return pl.ds(pl.multiple_of(which * width, 128), width)


def chain(planes):
    f_place, t_place = lax.axis_index("fsdp"), lax.axis_index("tp")
    plane = f_place // 2
    above = {"fsdp": f_place + 2, "tp": t_place}
    below = {"fsdp": f_place - 2, "tp": t_place}
    return plane, above, below, plane < planes - 1, plane > 0


class PlaneGather:
    def __init__(self, planes, whole, send_sems, recv_sems):
        self.planes, self.whole, self.send_sems, self.recv_sems = planes, whole, send_sems, recv_sems
        self.plane, above, below, has_above, has_below = chain(planes)
        self.side = lax.axis_index("fsdp") % 2
        self.devices, self.has_after = (above, below), (has_above, has_below)

    def spot(self, plane, piece):
        return self.whole.at[plane, self.side if piece == 0 else 1 - self.side]

    def copy(self, way, step, piece, back):
        ref = self.spot(self.plane - back if way == 0 else self.plane + back, piece)
        return pltpu.make_async_remote_copy(
            src_ref=ref,
            dst_ref=ref,
            send_sem=self.send_sems.at[way, step, piece],
            recv_sem=self.recv_sems.at[way, step, piece],
            device_id=self.devices[way],
            device_id_type=MESH,
        )

    def exists(self, way, back):
        return self.plane >= back if way == 0 else self.plane + back < self.planes

    def send(self, step, piece):
        for way in range(2):

            @pl.when(self.has_after[way] & self.exists(way, step - 1))
            def _():
                self.copy(way, step, piece, step - 1).start()

    def receive(self, step, piece):
        for way in range(2):

            @pl.when(self.exists(way, step))
            def _():
                self.copy(way, step, piece, step).wait_recv()

    def drain(self):
        for step in range(1, self.planes):
            for piece in range(2):
                for way in range(2):

                    @pl.when(self.has_after[way] & self.exists(way, step - 1))
                    def _():
                        self.copy(way, step, piece, step - 1).wait_send()


def gather_kernel(
    planes,
    input_ref,
    segment_ref,
    affine_ref,
    w_out_ref,
    w_fc2_ref,
    given_ref,
    qkv_ref,
    fc1_ref,
    normed_all,
    given_all,
    qo_all,
    head_all,
    fc1_block,
    fc2_kept_ref,
    fc2_going_ref,
    bound_ref,
    cos_ref,
    sin_ref,
    given_sum_ref,
    normed_ref,
    given_vmem,
    out_ref,
    send_sems,
    recv_sems,
    plane_send_sems,
    plane_recv_sems,
    head_send_sems,
    head_recv_sems,
):
    side, chip, core, over_x, over_y, over_core = neighbours()
    plane, above, below, has_above, has_below = chain(planes)
    rows = input_ref.shape[0]
    cut = rows // 2
    length = segment_ref.shape[1]
    out_ref[...] = w_out_ref[...].T
    zeros = length - jnp.sum(segment_ref[...], axis=1, keepdims=True)
    bound_ref[side] = jnp.broadcast_to(zeros.astype(wide), bound_ref.shape[1:])
    greet(
        (over_x, True), (over_y, True), (over_core, True), (above, has_above), (below, has_below)
    )
    copies = Copies(send_sems, recv_sems)

    width = out_ref.shape[1] // 2
    qo = PlaneGather(planes, qo_all, plane_send_sems, plane_recv_sems)
    qo_kept, qo_came = [], []
    for part in range(4):
        source = qkv_ref.at[part] if part < 3 else out_ref
        target = qo_all.at[plane, side, :, pl.ds(part * width, width)]
        qo_kept.append(copies.local(source.at[:, half(side, width)], target))
        qo_came.append(copies.remote(source.at[:, half(1 - side, width)], target, over_x))
    bounds = copies.remote(bound_ref.at[side], bound_ref.at[side], over_x)
    mine = [whole.at[side, chip, core] for whole in (normed_all, given_all)]
    y_slot = [whole.at[side, 1 - chip, core] for whole in (normed_all, given_all)]
    x_slot = [whole.at[1 - side, chip, core] for whole in (normed_all, given_all)]
    y_given = copies.remote(given_ref, mine[1], over_y)
    for copy in qo_kept:
        copy.wait()
    qo.send(1, 0)

    tokens = input_ref[...].astype(wide)
    normed_ref[...] = layer_norm(
        tokens, affine_ref[0:1].astype(wide), affine_ref[1:2].astype(wide)
    ).astype(narrow)
    kept = [copies.local(normed_ref, mine[0]), copies.local(given_ref, mine[1])]
    own_given = copies.local(given_ref, given_vmem)
    last = [
        copies.remote(normed_ref, mine[0], over_core),
        copies.remote(given_ref, mine[1], over_core),
    ]
    ff_width, head_width = fc1_ref.shape[1] // 2, head_all.shape[3]
    head = PlaneGather(planes, head_all, head_send_sems, head_recv_sems)

    def fc1_head(which):
        return fc1_ref.at[:, pl.ds(pl.multiple_of(which * ff_width, 128), head_width)]

    def fc1_tail(which):
        start = pl.multiple_of(which * ff_width + head_width, 128)
        return fc1_ref.at[:, pl.ds(start, ff_width - head_width)]

    head_kept = copies.local(fc1_head(side), head_all.at[plane, side])
    kept.append(copies.local(fc1_tail(side), fc1_block.at[side]))
    for copy in qo_came:
        copy.wait_recv()
    qo.send(1, 1)
    x_normed = copies.remote(normed_ref, mine[0], over_x)
    y_normed = copies.remote(normed_ref, mine[0], over_y)
    head_came = copies.remote(fc1_head(1 - side), head_all.at[plane, side], over_x)

    def forward(gather, step, piece):
        gather.receive(step - 1, piece)
        gather.send(step, piece)

    if planes > 2:
        forward(qo, 2, 0)
    bounds.wait_recv()
    step = min(256, length)
    frequency, sign = lane_constants()

    def tables(i, carry):
        here = pl.ds(pl.multiple_of(i * step, 8), step)
        sequence, first = i // (length // step), (i % (length // step)) * step
        place = (first + lax.broadcasted_iota(jnp.int32, (step, 1), 0)).astype(wide)
        bound = bound_ref[sequence, 0:1, 0:1]
        angles = (place - jnp.where(place >= bound, bound, 0.0)) * frequency
        cos_ref[here] = jnp.cos(angles)
        sin_ref[here] = jnp.sin(angles) * sign
        return carry

    lax.fori_loop(0, 2 * length // step, tables, 0)
    if planes > 2:
        forward(qo, 2, 1)
    ff_rows = w_fc2_ref.shape[0] // 2
    for target, which in ((fc2_kept_ref, side), (fc2_going_ref, 1 - side)):
        target[...] = w_fc2_ref[pl.ds(pl.multiple_of(which * ff_rows, 128), ff_rows)].T
    own_given.wait()
    given_sum_ref[...] = jnp.sum(given_vmem[...].astype(wide), axis=0, keepdims=True)
    if planes > 3:
        forward(qo, 3, 0)
    x_normed.wait_recv()
    x_given = copies.remote(given_ref, mine[1], over_x)
    corner = [[copies.remote(x_slot[0], x_slot[0], over_y)]]
    last.append(copies.remote(x_slot[0], x_slot[0], over_core))
    if planes > 3:
        forward(qo, 3, 1)
    for k in range(4, planes):
        for piece in range(2):
            forward(qo, k, piece)
    head_kept.wait()
    head.send(1, 0)
    head_came.wait_recv()
    head.send(1, 1)
    y_given.wait_recv()
    last.append(copies.remote(y_slot[1], y_slot[1], over_core))
    y_normed.wait_recv()
    last.append(copies.remote(y_slot[0], y_slot[0], over_core))
    x_given.wait_recv()
    part = y_slot[1].at[pl.ds(0, cut)]
    other_part = x_slot[1].at[pl.ds(cut, rows - cut)]
    corner.append([copies.remote(part, part, over_x), copies.remote(other_part, other_part, over_y)])
    last.append(copies.remote(fc1_tail(1 - side), fc1_block.at[side], over_x))
    last.append(copies.remote(x_slot[1], x_slot[1], over_core))
    for k in range(2, planes):
        for piece in range(2):
            forward(head, k, piece)
    for whole, parts in zip((normed_all, given_all), corner):
        for copy in parts:
            copy.wait_recv()
        slot = whole.at[1 - side, 1 - chip, core]
        last.append(copies.remote(slot, slot, over_core))
    for piece in range(2):
        qo.receive(planes - 1, piece)
        head.receive(planes - 1, piece)
    for copy in kept:
        copy.wait()
    for copy in copies.started:
        copy.wait_send()
    qo.drain()
    head.drain()
    for copy in last:
        copy.wait_recv()


def gather_tokens(planes, inputs, segments, affine, given, w_qkv, w_out, fc1, w_fc2):
    mine, rows, lanes = inputs.shape[0], fc1.shape[0], 2 * HEAD_DIM
    tokens, length = 8 * mine, segments.shape[1]
    columns = 2 * w_out.shape[0]
    whole = jax.ShapeDtypeStruct((2, 2, 2, mine, D), narrow)
    head = max(128, 3 * fc1.shape[1] // 16)
    block = jax.ShapeDtypeStruct((2, rows, fc1.shape[1] // 2 - head), narrow)
    table = jax.ShapeDtypeStruct((2 * length, lanes), wide)
    weights = jax.ShapeDtypeStruct((planes, 2, rows, columns), narrow)
    anywhere, vmem = pl.BlockSpec(memory_space=pl.ANY), pl.BlockSpec(memory_space=pltpu.VMEM)
    ff_half = jax.ShapeDtypeStruct((rows, w_fc2.shape[0] // 2), narrow)
    outs = pl.pallas_call(
        functools.partial(gather_kernel, planes),
        in_specs=[vmem] * 5 + [anywhere] * 3,
        out_specs=[anywhere] * 5 + [vmem] * 6,
        out_shape=[
            whole,
            whole,
            weights,
            jax.ShapeDtypeStruct((planes, 2, rows, head), narrow),
            block,
            ff_half,
            ff_half,
            jax.ShapeDtypeStruct((2, 8, 128), wide),
            table,
            table,
            jax.ShapeDtypeStruct((1, D), wide),
        ],
        scratch_shapes=[
            pltpu.VMEM((mine, D), narrow),
            pltpu.VMEM((mine, D), narrow),
            pltpu.VMEM((rows, w_out.shape[0]), narrow),
            pltpu.SemaphoreType.DMA((32,)),
            pltpu.SemaphoreType.DMA((32,)),
            pltpu.SemaphoreType.DMA((2, planes, 2)),
            pltpu.SemaphoreType.DMA((2, planes, 2)),
            pltpu.SemaphoreType.DMA((2, planes, 2)),
            pltpu.SemaphoreType.DMA((2, planes, 2)),
        ],
        compiler_params=pltpu.CompilerParams(
            collective_id=1, has_side_effects=True, vmem_limit_bytes=VMEM
        ),
        name="gather_tokens",
    )(inputs, segments, affine, w_out, w_fc2, given, w_qkv, fc1)
    normed_all, given_all, qo_all, head_all = outs[:4]
    return (
        normed_all.reshape(tokens, D),
        given_all.reshape(tokens, D),
        qo_all.reshape(D, columns),
        head_all.reshape(D, head),
    ) + tuple(outs[4:])


def scatter_kernel(planes, which, *refs):
    lefts = sorted(set(which))
    n_left, n_right = len(lefts), len(which)
    left_refs, right_refs = refs[:n_left], refs[n_left : n_left + n_right]
    (
        fc1_head_ref,
        fc1_tail_ref,
        bias_ref,
        kept_ref,
        came_ref,
        out_ref,
        weight_all,
        active_all,
        slope_all,
        grad_all,
        left_vmem,
        own,
        turned,
        going,
        came,
        active_stage,
        slope_stage,
        grad_stage,
        load_sems,
        send_sems,
        recv_sems,
        store_sems,
    ) = refs[n_left + n_right :]
    side = lax.axis_index("fsdp") % 2
    plane, above, below, has_above, has_below = chain(planes)
    devices, has_after, has_before = (above, below), (has_above, has_below), (has_below, has_above)
    group, width = own.shape[1], right_refs[0].shape[1]
    rows, tokens = group // 2, right_refs[0].shape[0]

    def load(j):
        return [
            pltpu.make_async_copy(
                left_refs[i].at[:, pl.ds(pl.multiple_of(j * group, 128), group)],
                left_vmem.at[i, j],
                load_sems.at[i, j],
            )
            for i in range(n_left)
        ]

    def order(k):
        return jnp.where(plane < planes // 2, planes - 1 - k, k)

    for k in range(planes):
        for copy in load(order(k)):
            copy.start()
    greet((above, has_above), (below, has_below))
    own_weight = [
        pltpu.make_async_copy(ref, weight_all.at[plane, at], store_sems.at[3, piece])
        for piece, (ref, at) in enumerate(((kept_ref, side), (came_ref, 1 - side)))
    ]

    def depth(way):
        return plane if way == 0 else planes - 1 - plane

    def named(way, block):
        return block if way == 0 else planes - 1 - block

    def is_weight(at, number):
        return number <= at + 1

    def weight_block(at, number):
        return at - number + 1

    def sum_block(at, number):
        return planes + 1 + at - number

    def weight_copy(way, number, at, piece):
        j = named(way, weight_block(at, number))
        ref = weight_all.at[j, side if piece == 0 else 1 - side]
        return pltpu.make_async_remote_copy(
            src_ref=(kept_ref, came_ref)[piece] if number == 1 else ref,
            dst_ref=ref,
            send_sem=send_sems.at[way, number, piece],
            recv_sem=recv_sems.at[way, number, piece],
            device_id=devices[way],
            device_id_type=MESH,
        )

    cut = own.shape[0] // 2
    spans = (slice(0, cut), slice(cut, 2 * cut))

    def sum_copy(way, number, at, receiver, arriving, piece):
        j = named(way, sum_block(at, number))
        spot = j if way == 0 else jnp.where(j == receiver, planes, j)
        here = pl.ds(piece * cut, cut)
        return j, spot, pltpu.make_async_remote_copy(
            src_ref=came.at[spot, here] if arriving else going.at[j, here],
            dst_ref=came.at[spot, here],
            send_sem=send_sems.at[way, number, 2 + piece],
            recv_sem=recv_sems.at[way, number, 2 + piece],
            device_id=devices[way],
            device_id_type=MESH,
        )

    def next_plane(way):
        return plane + 1 if way == 0 else plane - 1

    def finish_send(way, number, piece):
        at = depth(way)

        @pl.when(has_after[way] & is_weight(at, number))
        def _():
            weight_copy(way, number, at, piece).wait_send()

        @pl.when(has_after[way] & jnp.logical_not(is_weight(at, number)))
        def _():
            sum_copy(way, number, at, next_plane(way), False, piece)[2].wait_send()

    def take(way, number, piece):
        at = depth(way) - 1

        @pl.when(has_before[way] & is_weight(at, number))
        def _():
            weight_copy(way, number, at, piece).wait_recv()

        @pl.when(has_before[way] & jnp.logical_not(is_weight(at, number)))
        def _():
            j, spot, copy = sum_copy(way, number, at, plane, True, piece)
            copy.wait_recv()
            here = spans[piece]

            @pl.when(j == plane)
            def _():
                own[here] += came[spot, here].astype(wide)

            @pl.when(j != plane)
            def _():
                going[j, here] = (
                    going[j, here].astype(wide) + came[spot, here].astype(wide)
                ).astype(narrow)

    def give(way, number, piece):
        at = depth(way)

        @pl.when(has_after[way] & is_weight(at, number))
        def _():
            weight_copy(way, number, at, piece).start()

        @pl.when(has_after[way] & jnp.logical_not(is_weight(at, number)))
        def _():
            sum_copy(way, number, at, next_plane(way), False, piece)[2].start()

    step = slope_stage.shape[1]
    blocks = tokens // step

    def turn(i, carry):
        here = pl.ds(pl.multiple_of(i * step, 128), step)
        for number, right_ref in enumerate(right_refs):
            turned[number * width : (number + 1) * width, here] = right_ref[here].T
        return carry

    def multiply(k):
        j = order(k)
        for copy in load(j):
            copy.wait()
        for i in range(n_left):
            numbers = [number for number, left in enumerate(which) if left == lefts[i]]
            here = slice(numbers[0] * width, (numbers[-1] + 1) * width)
            block = nn(turned[here], left_vmem[i, j])
            going[j, here] = block.astype(narrow)

            @pl.when(j == plane)
            def _():
                own[here] = block

    def store_hidden(i, slot):
        here = pl.ds(pl.multiple_of(i * step, 16), step)
        return [
            pltpu.make_async_copy(slope_stage.at[slot], slope_all.at[here], store_sems.at[0, slot]),
            pltpu.make_async_copy(active_stage.at[slot], active_all.at[here], store_sems.at[1, slot]),
        ]

    def hidden_units(i, carry):
        here = pl.ds(pl.multiple_of(i * step, 128), step)
        slot = i % 2
        parts = []
        for part_ref in (fc1_head_ref, fc1_tail_ref):
            part = nn(left_vmem[0, 0, here], part_ref[0:group])
            for j in range(1, planes):
                part += nn(left_vmem[0, j, here], part_ref[j * group : (j + 1) * group])
            parts.append(part)
        hidden = bias_ref[...] + jnp.concatenate(parts, axis=1)
        squared = hidden * hidden
        inner = jnp.tanh(0.7978845608028654 * hidden * (1.0 + 0.044715 * squared))
        half_sum = 0.5 * (1.0 + inner)
        active = (hidden * half_sum).astype(narrow)

        @pl.when(i >= 2)
        def _():
            for copy in store_hidden(i - 2, slot):
                copy.wait()

        active_stage[slot] = active
        slope_stage[slot] = half_sum + hidden * (0.5 * (1.0 - inner * inner)) * (
            0.7978845608028654 * (1.0 + 3.0 * 0.044715 * squared)
        )
        for copy in store_hidden(i, slot):
            copy.start()
        turned[:, here] = active.T
        return carry

    def store_grad(j, slot):
        return pltpu.make_async_copy(grad_stage.at[slot], grad_all.at[j], store_sems.at[2, slot])

    def fc2_gradient(j, carry):
        slot = j % 2

        @pl.when(j >= 2)
        def _():
            store_grad(j - 2, slot).wait()

        block = nn(turned[...], left_vmem[n_left - 1, j]).astype(narrow)
        for number in range(2):
            grad_stage[slot, number] = block[:, number * rows : (number + 1) * rows]
        store_grad(j, slot).start()
        return carry

    for piece in range(2):
        for way in range(2):
            give(way, 1, piece)
    for copy in own_weight:
        copy.start()
    lax.fori_loop(0, blocks, turn, 0)
    multiply(0)
    multiply(1)

    work = [lambda: [multiply(k) for k in range(2, planes)]]
    parts = min(4, blocks)
    for part in range(parts):
        work.append(
            functools.partial(
                lax.fori_loop, part * blocks // parts, (part + 1) * blocks // parts, hidden_units, 0
            )
        )
    for part in range(2):
        work.append(
            functools.partial(
                lax.fori_loop, part * planes // 2, (part + 1) * planes // 2, fc2_gradient, 0
            )
        )
    for number in range(2, planes + 1):
        for piece in range(2):
            for way in range(2):
                take(way, number - 1, piece)
                finish_send(way, number - 1, piece)
                give(way, number, piece)
            if work:
                work.pop(0)()
    for part in work:
        part()
    for piece in range(2):
        for way in range(2):
            take(way, planes, piece)
    for number in range(2):
        out_ref[number] = own[:, number * rows : (number + 1) * rows].astype(narrow)
    for piece in range(2):
        for way in range(2):
            finish_send(way, planes, piece)
    for slot in range(2):
        for copy in store_hidden(blocks - 2 + slot, slot) + [store_grad(planes - 2 + slot, slot)]:
            copy.wait()
    for copy in own_weight:
        copy.wait()


def backward_step(planes, lefts, rights, which, fc1, bias, weight, collective_id):
    tokens, width = rights[0].shape
    group, columns, hidden = D // planes, width * len(rights), bias.shape[1]
    rows, step = group // 2, min(256, tokens // 2)
    anywhere, vmem = pl.BlockSpec(memory_space=pl.ANY), pl.BlockSpec(memory_space=pltpu.VMEM)
    total, weight_all, active, slope, grad = pl.pallas_call(
        functools.partial(scatter_kernel, planes, which),
        in_specs=[anywhere] * len(lefts) + [vmem] * (len(rights) + 3) + [anywhere] * 2,
        out_specs=[vmem] + [anywhere] * 4,
        out_shape=[
            jax.ShapeDtypeStruct((2, columns, rows), narrow),
            jax.ShapeDtypeStruct((planes, 2, rows, weight[0].shape[1]), narrow),
            jax.ShapeDtypeStruct((tokens, hidden), narrow),
            jax.ShapeDtypeStruct((tokens, hidden), wide),
            jax.ShapeDtypeStruct((planes, 2, hidden, rows), narrow),
        ],
        scratch_shapes=[
            pltpu.VMEM((len(lefts), planes, tokens, group), narrow),
            pltpu.VMEM((columns, group), wide),
            pltpu.VMEM((columns, tokens), narrow),
            pltpu.VMEM((planes, columns, group), narrow),
            pltpu.VMEM((planes + 1, columns, group), narrow),
            pltpu.VMEM((2, step, hidden), narrow),
            pltpu.VMEM((2, step, hidden), wide),
            pltpu.VMEM((2, 2, hidden, rows), narrow),
            pltpu.SemaphoreType.DMA((len(lefts), planes)),
            pltpu.SemaphoreType.DMA((2, planes + 1, 4)),
            pltpu.SemaphoreType.DMA((2, planes + 1, 4)),
            pltpu.SemaphoreType.DMA((4, 2)),
        ],
        compiler_params=pltpu.CompilerParams(
            collective_id=collective_id, has_side_effects=True, vmem_limit_bytes=VMEM
        ),
        cost_estimate=pl.CostEstimate(
            flops=40 * tokens * D * columns, bytes_accessed=2 * tokens * D, transcendentals=0
        ),
        name="backward_step",
    )(*lefts, *rights, *fc1, bias, *weight)
    return total, weight_all.reshape(D, weight[0].shape[1]), active, slope, grad


def project_kernel(normed_ref, given_ref, in_ref, out_ref, bias_ref, projected_ref, given_attn_ref):
    projected_ref[...] = nn(normed_ref[...], in_ref[...]) + bias_ref[...]
    given_attn_ref[...] = nn(given_ref[...], out_ref[...]).astype(narrow)


def project(normed, given, weights, bias):
    tokens, width = normed.shape[0], weights.shape[1] // 4
    block = min(512, tokens)
    row = pl.BlockSpec((block, D), lambda i: (i, 0))
    return pl.pallas_call(
        project_kernel,
        grid=(tokens // block,),
        in_specs=[
            row,
            row,
            pl.BlockSpec((D, 3 * width), lambda i: (0, 0)),
            pl.BlockSpec((D, width), lambda i: (0, 3)),
            pl.BlockSpec((1, 3 * width), lambda i: (0, 0)),
        ],
        out_specs=[
            pl.BlockSpec((block, 3 * width), lambda i: (i, 0)),
            pl.BlockSpec((block, width), lambda i: (i, 0)),
        ],
        out_shape=[
            jax.ShapeDtypeStruct((tokens, 3 * width), wide),
            jax.ShapeDtypeStruct((tokens, width), narrow),
        ],
        compiler_params=pltpu.CompilerParams(vmem_limit_bytes=VMEM),
        cost_estimate=pl.CostEstimate(
            flops=8 * tokens * D * width, bytes_accessed=8 * tokens * D, transcendentals=0
        ),
        name="project",
    )(normed, given, weights, weights, bias)


def reduce_kernel(terms, n_left, n_right, has_extra, n_sums, *refs):
    left_refs, right_refs = refs[:n_left], refs[n_left : n_left + n_right]
    rest = list(refs[n_left + n_right :])
    extra_ref = rest.pop(0) if has_extra else None
    out_ref = rest.pop(0)
    extra_came = rest.pop(0) if has_extra else None
    sum_refs = [rest.pop(0) for _ in range(n_sums)]
    (
        core_going,
        core_came,
        sums,
        x_going,
        x_came,
        y_going,
        y_came,
        send_sems,
        recv_sems,
    ) = rest
    side, chip, core, over_x, over_y, over_core = neighbours()
    mine, columns = out_ref.shape
    cut = columns // 4 if has_extra else columns // 2
    first, second = slice(0, cut), slice(cut, columns)
    greet((over_x, True), (over_y, True), (over_core, True))

    if has_extra:
        extra = pltpu.make_async_remote_copy(
            src_ref=extra_ref.at[1 - side],
            dst_ref=extra_came,
            send_sem=send_sems.at[0, 4],
            recv_sem=recv_sems.at[0, 4],
            device_id=over_x,
            device_id_type=MESH,
        )
        extra.start()

    def copy(lane, number):
        going, came, other = (
            (core_going, core_came, over_core),
            (x_going, x_came, over_x),
            (y_going, y_came, over_y),
        )[lane]
        if lane == 0:
            here = number
        else:
            here = (number, slice(None), first if (lane == 1) == (number < 2) else second)
        return pltpu.make_async_remote_copy(
            src_ref=going.at[here],
            dst_ref=came.at[here],
            send_sem=send_sems.at[lane, number],
            recv_sem=recv_sems.at[lane, number],
            device_id=other,
            device_id_type=MESH,
        )

    def product(number):
        here = pl.ds(pl.multiple_of(number * mine, 16), mine)
        total = None
        for left, start, width, right, column in terms:
            part = nt(
                left_refs[left][here, start : start + width],
                right_refs[right][:, column : column + width],
            )
            total = part if total is None else total + part
        return total

    def quarter(q, carry):
        its_side = jnp.where(q < 2, 1 - side, side)
        its_chip = jnp.where(q % 2 == 0, 1 - chip, chip)
        base = (its_side * 2 + its_chip) * 2
        core_going[q] = product(base + 1 - core).astype(narrow)
        copy(0, q).start()
        block = product(base + core)
        copy(0, q).wait_recv()
        sums[q] = block + core_came[q].astype(wide)

        for number in range(2):

            @pl.when(q == number)
            def _():
                x_going[number, :, first] = sums[number, :, first].astype(narrow)
                copy(1, number).start()

            @pl.when(q == 2 * number)
            def _():
                y_going[number, :, second] = sums[2 * number, :, second].astype(narrow)
                copy(2, number).start()

        return carry

    lax.fori_loop(0, 4, quarter, 0)
    copy(1, 0).wait_recv()
    y_going[2, :, first] = (sums[2, :, first] + x_came[0, :, first].astype(wide)).astype(narrow)
    copy(2, 2).start()
    copy(2, 0).wait_recv()
    x_going[2, :, second] = (sums[1, :, second] + y_came[0, :, second].astype(wide)).astype(narrow)
    copy(1, 2).start()
    for left_ref, sum_ref in zip(left_refs, sum_refs):
        sum_ref[...] = jnp.zeros_like(sum_ref)

        def add(i, carry):
            here = pl.ds(pl.multiple_of(i * mine, 16), mine)
            sum_ref[...] += jnp.sum(left_ref[here].astype(wide), axis=0, keepdims=True)
            return carry

        lax.fori_loop(0, left_ref.shape[0] // mine, add, 0)
    copy(1, 1).wait_recv()
    out_ref[:, first] = sums[3, :, first] + x_came[1, :, first].astype(wide)
    copy(2, 1).wait_recv()
    out_ref[:, second] = sums[3, :, second] + y_came[1, :, second].astype(wide)
    copy(2, 2).wait_recv()
    out_ref[:, first] += y_came[2, :, first].astype(wide)
    copy(1, 2).wait_recv()
    out_ref[:, second] += x_came[2, :, second].astype(wide)
    if has_extra:
        extra.wait()
    for q in range(4):
        copy(0, q).wait_send()
    for lane in (1, 2):
        for number in range(3):
            copy(lane, number).wait_send()


def distinct(values):
    kept = []
    for value in values:
        if not any(value is other for other in kept):
            kept.append(value)
    return kept


def place_of(value, values):
    return next(i for i, other in enumerate(values) if other is value)


def reduce_products(mine, terms, collective_id, extra=None, sums=False):
    lefts = distinct([term[0] for term in terms])
    rights = distinct([term[3] for term in terms])
    places = tuple(
        (place_of(a, lefts), start, width, place_of(w, rights), column)
        for a, start, width, w, column in terms
    )
    extras = [] if extra is None else [extra]
    totals = [jax.ShapeDtypeStruct((1, a.shape[1]), wide) for a in lefts] if sums else []
    tokens, depth = terms[0][0].shape[0], sum(term[2] for term in terms)
    anywhere, vmem = pl.BlockSpec(memory_space=pl.ANY), pl.BlockSpec(memory_space=pltpu.VMEM)
    return pl.pallas_call(
        functools.partial(
            reduce_kernel,
            places,
            len(lefts),
            len(rights),
            extra is not None,
            len(lefts) if sums else 0,
        ),
        in_specs=[vmem] * (len(lefts) + len(rights)) + [anywhere] * len(extras),
        out_specs=[vmem] + [anywhere] * len(extras) + [vmem] * len(totals),
        out_shape=[jax.ShapeDtypeStruct((mine, D), wide)]
        + [jax.ShapeDtypeStruct(e.shape[1:], e.dtype) for e in extras]
        + totals,
        scratch_shapes=[
            pltpu.VMEM((4, mine, D), narrow),
            pltpu.VMEM((4, mine, D), narrow),
            pltpu.VMEM((4, mine, D), wide),
            pltpu.VMEM((3, mine, D), narrow),
            pltpu.VMEM((3, mine, D), narrow),
            pltpu.VMEM((3, mine, D), narrow),
            pltpu.VMEM((3, mine, D), narrow),
            pltpu.SemaphoreType.DMA((3, 5)),
            pltpu.SemaphoreType.DMA((3, 5)),
        ],
        compiler_params=pltpu.CompilerParams(
            collective_id=collective_id, has_side_effects=True, vmem_limit_bytes=VMEM
        ),
        cost_estimate=pl.CostEstimate(
            flops=8 * tokens * depth * D, bytes_accessed=2 * depth * (tokens + D), transcendentals=0
        ),
        name="reduce_products",
    )(*lefts, *rights, *extras)


def solution(mesh):
    nf = mesh.shape["fsdp"]
    nt_axis = mesh.shape["tp"]
    columns_of_planes = [list(range(side, nf, 2)) for side in range(2)]
    swap_f = [(f, f ^ 1) for f in range(nf)]
    swap_core = [(t, t ^ 1) for t in range(nt_axis)]
    swap_chip = [(t, t ^ 2) for t in range(nt_axis)]

    def send_x(v):
        return lax.ppermute(v, "fsdp", swap_f)

    def send_y(v):
        return lax.ppermute(v, "tp", swap_chip)

    def send_core(v):
        return lax.ppermute(v, "tp", swap_core)

    def gather_planes(block):
        block = block.reshape(block.shape[0] * block.shape[1], block.shape[2])
        return lax.all_gather(
            block, "fsdp", axis=0, tiled=True, axis_index_groups=columns_of_planes
        )

    def local(
        inputs,
        segments,
        ln_gain,
        ln_bias,
        w_qkv,
        b_qkv,
        w_out,
        b_out,
        w_fc1,
        b_fc1,
        w_fc2,
        b_fc2,
        cotangent,
    ):
        f_place = lax.axis_index("fsdp")
        t_place = lax.axis_index("tp")
        side = f_place % 2
        chip, core = t_place // 2, t_place % 2
        length = segments.shape[1]
        mine = inputs.shape[0]
        rows = w_fc1.shape[0]
        half_qkv, half_ff = w_qkv.shape[2] // 2, w_fc1.shape[1] // 2

        def pick(v, index, axis=0):
            return lax.dynamic_index_in_dim(v, index, axis, keepdims=False)

        def in_order(kept, came):
            return jnp.where(side == 0, jnp.stack([kept, came]), jnp.stack([came, kept]))

        def sum_planes(grads):
            return lax.psum_scatter(
                grads.astype(narrow),
                "fsdp",
                scatter_dimension=0,
                tiled=True,
                axis_index_groups=columns_of_planes,
            )

        def halves_of(kept, came):
            return in_order(kept, came).astype(wide)

        def reduce_all(v):
            for axis, size in (("tp", nt_axis), ("fsdp", nf)):
                bit = 1
                while bit < size:
                    v = v + lax.ppermute(v, axis, [(i, i ^ bit) for i in range(size)])
                    bit *= 2
            return v

        (
            normed,
            grad_rows,
            full_qo,
            fc1_head,
            fc1_block,
            fc2_kept,
            fc2_going,
            bounds,
            cosine,
            sine,
            cotangent_sum,
        ) = gather_tokens(
            nf // 2,
            inputs,
            segments,
            jnp.stack([ln_gain, ln_bias]),
            cotangent,
            w_qkv,
            w_out,
            w_fc1,
            w_fc2,
        )
        fc1_tail = gather_planes(fc1_block)
        fc2_came = send_x(fc2_going)
        bias_qkv = lax.dynamic_slice_in_dim(b_qkv, side * half_qkv, half_qkv, axis=1)
        bias_fc1 = lax.dynamic_slice_in_dim(b_fc1, side * half_ff, half_ff, axis=0)

        projected, grad_mixed = project(
            normed, grad_rows, full_qo, bias_qkv.astype(wide).reshape(1, 3 * half_qkv)
        )
        mixed, grad_q, grad_k, grad_v = attention(
            bounds, cosine, sine, projected, grad_mixed, length
        )
        sum_qo, full_fc2, active_low, slope, grad_w2 = backward_step(
            nf // 2,
            [normed, grad_rows],
            [grad_q, grad_k, grad_v, mixed],
            (0, 0, 0, 1),
            (fc1_head, fc1_tail),
            bias_fc1.astype(wide).reshape(1, half_ff),
            (fc2_kept, fc2_came),
            2,
        )
        (
            grad_q, grad_k, grad_v, sum_qo, inputs, ln_gain, ln_bias, b_out, b_fc2, cotangent, cotangent_sum
        ) = lax.optimization_barrier(
            (grad_q, grad_k, grad_v, sum_qo, inputs, ln_gain, ln_bias, b_out, b_fc2, cotangent, cotangent_sum)
        )
        tokens_in = inputs.astype(wide)
        _, norm_back = jax.vjp(
            layer_norm, tokens_in, ln_gain.astype(wide), ln_bias.astype(wide)
        )
        total_fc2 = sum_planes(grad_w2.reshape(-1, rows))
        grad_hidden = (nn(grad_rows, full_fc2) * slope).astype(narrow)
        grad_w1 = tn(normed, grad_hidden).astype(narrow)
        mixed, grad_w1 = lax.optimization_barrier((mixed, grad_w1))
        came_qo = send_x(pick(sum_qo, 1 - side))
        (branch_local,) = reduce_products(
            mine,
            [(mixed, 0, half_qkv, full_qo, 3 * half_qkv), (active_low, 0, half_ff, full_fc2, 0)],
            4,
        )
        total_fc2, grad_hidden, grad_w1, branch_local = lax.optimization_barrier(
            (total_fc2, grad_hidden, grad_w1, branch_local)
        )
        total_fc1 = sum_planes(grad_w1)
        total_fc2 = total_fc2.reshape(2, half_ff, rows)
        head = fc1_head.shape[1]
        grad_normed, came_fc2, sum_q, sum_k, sum_v, sum_hidden = reduce_products(
            mine,
            [
                (grad_q, 0, half_qkv, full_qo, 0),
                (grad_k, 0, half_qkv, full_qo, half_qkv),
                (grad_v, 0, half_qkv, full_qo, 2 * half_qkv),
                (grad_hidden, 0, head, fc1_head, 0),
                (grad_hidden, head, half_ff - head, fc1_tail, 0),
            ],
            3,
            extra=total_fc2,
            sums=True,
        )
        sum_qo, came_qo, grad_normed = lax.optimization_barrier((sum_qo, came_qo, grad_normed))
        sum_qo = halves_of(pick(sum_qo, side), came_qo)
        sum_fc2 = halves_of(pick(total_fc2, side), came_fc2)
        outputs = (tokens_in + branch_local + b_out.astype(wide) + b_fc2.astype(wide)).astype(narrow)
        grad_tokens, grad_gain, grad_offset = norm_back(grad_normed)
        grad_tokens = grad_tokens + cotangent.astype(wide)

        grad_w_qkv = sum_qo[:, : 3 * half_qkv].reshape(2, 3, half_qkv, rows)
        grad_w_qkv = grad_w_qkv.transpose(1, 3, 0, 2).reshape(3, rows, 2 * half_qkv)
        grad_w_out = sum_qo[:, 3 * half_qkv :].reshape(2 * half_qkv, rows)
        grad_w_fc2 = sum_fc2.reshape(2 * half_ff, rows)

        anchor = jnp.zeros((), jnp.int32)
        bias_qkv_full = lax.dynamic_update_slice(
            jnp.zeros((3, D), wide),
            jnp.concatenate([sum_q, sum_k, sum_v], axis=0),
            (anchor, (2 * t_place + side) * half_qkv),
        )
        bias_fc1_full = lax.dynamic_update_slice(
            jnp.zeros((FF,), wide),
            sum_hidden.reshape(-1),
            ((2 * t_place + side) * half_ff,),
        )
        small = reduce_all(
            jnp.concatenate(
                [bias_qkv_full.reshape(-1), bias_fc1_full, grad_gain, grad_offset, cotangent_sum.reshape(-1)]
            ).reshape(-1, 128)
        ).reshape(-1)
        total_fc1, outputs, grad_tokens, grad_w_qkv, grad_w_out, grad_w_fc2 = (
            lax.optimization_barrier(
                (total_fc1, outputs, grad_tokens, grad_w_qkv, grad_w_out, grad_w_fc2)
            )
        )
        parts = total_fc1.reshape(2, rows, total_fc1.shape[1])
        kept, came = pick(parts, side).astype(wide), send_x(pick(parts, 1 - side)).astype(wide)
        grad_w_fc1 = jnp.where(
            side == 0,
            jnp.concatenate([kept, came], axis=1),
            jnp.concatenate([came, kept], axis=1),
        )
        total_qkv = small[: 3 * D].reshape(3, D)
        total_b_fc1 = small[3 * D : 3 * D + FF]
        total_gain, total_offset, total_out = small[3 * D + FF :].reshape(3, D)
        return (
            outputs,
            grad_tokens,
            total_gain,
            total_offset,
            grad_w_qkv,
            total_qkv,
            grad_w_out,
            total_out,
            grad_w_fc1,
            total_b_fc1,
            grad_w_fc2,
            total_out,
        )

    return jax.shard_map(
        local,
        mesh=mesh,
        in_specs=(
            P(("fsdp", "tp"), None),
            P("fsdp", None),
            P(),
            P(),
            P(None, "fsdp", "tp"),
            P(None, "tp"),
            P("tp", "fsdp"),
            P(),
            P("fsdp", "tp"),
            P("tp"),
            P("tp", "fsdp"),
            P(),
            P(("fsdp", "tp"), None),
        ),
        out_specs=(
            P(("fsdp", "tp"), None),
            P(("fsdp", "tp"), None),
            P(),
            P(),
            P(None, "fsdp", "tp"),
            P(),
            P("tp", "fsdp"),
            P(),
            P("fsdp", "tp"),
            P(),
            P("tp", "fsdp"),
            P(),
        ),
        check_vma=False,
    )
```
